256 devices in a mesh: dp: 64 (over y, z, core), tensor: 4 (over x).
Axes of the slice: x: 4, y: 4, z: 8, core: 2. Of those that a mesh axis runs over, the one named last changes fastest.
Arguments:
- acts: bfloat16 [65536, 1280], P('dp'), may hold values from -24 to 24, as said below
- cotangent: bfloat16 [65536, 5120], P('dp', 'tensor'), may hold values from -0.1875 to 0.1875
- error_prev: bfloat16 [81920, 5120], P('dp', 'tensor'), may hold values from -3 to 3
- q_prev: bfloat16 [64, 5120], P(None, 'tensor'), may hold values from -0.078125 to 0.078125
Outputs:
- error_new: bfloat16 [81920, 5120], P('dp', 'tensor')
- q_new: float32 [64, 5120], P(None, 'tensor')
The draws below stay inside these ranges and needn't reach their ends.
Inputs may be any that keep to these rules, and one draw needn't show every extreme that they name: `acts`: entries of the layer's inputs.
All inputs are finite; a program needn't handle non-finite values.
Results may differ from the reference program's by a relative error of at most 0.0058.
Values may be sent and summed in bfloat16 or wider, within the bound.
A program may use at most 64 MiB of HBM per device.

```python
import math
import jax
import jax.numpy as jnp
from jax import lax

ROWS = 1280
FFN = 5120
TOK_REP = 1024
RANK = 64
TOKENS = 65536
STACKED = 81920
N_DP = 64


def draw_acts(key, part):
    key = jax.random.fold_in(key, 11)
    key_base = jax.random.fold_in(key, 0)
    position = jnp.arange(ROWS, dtype=jnp.float32) / (ROWS - 1)
    scale = jnp.exp(position * math.log(3.0))
    base = jnp.clip(jax.random.normal(key_base, (TOKENS, ROWS), jnp.float32), -4.0, 4.0)
    return (base * scale[None, :]).astype(jnp.bfloat16)


def shard_levels(stream_key, dims, cuts, smallest, largest):
    factor_of, own = 1.0, jax.random.fold_in(stream_key, 6)
    for axis_at, blocks in cuts:
        heights = jnp.exp(jax.random.uniform(jax.random.fold_in(own, axis_at), (blocks,), jnp.float32, smallest / len(cuts), largest / len(cuts)))
        factor_of = factor_of * jnp.repeat(heights, dims[axis_at] // blocks).reshape([-1 if axis == axis_at else 1 for axis in range(len(dims))])
    return factor_of


def centred(rng, dims, deviation, limit, cuts=(), held_as=jnp.bfloat16):
    result = deviation * jax.random.normal(rng, dims, jnp.float32)
    if cuts:
        result = result * shard_levels(rng, dims, cuts, -0.22, 0.18)
    return jnp.clip(result, -limit, limit).astype(held_as)


def setup_inputs(seed: int = 0) -> dict:
    keys = jax.random.split(jax.random.key(seed), 5)
    acts = draw_acts(jax.random.fold_in(keys[4], 71), 0)
    cotangent = centred(keys[1], (TOKENS, FFN), TOK_REP ** -0.5, 0.1875, ((0, 64), (1, 4)))
    error_prev = centred(keys[2], (STACKED, FFN), 0.5, 3.0, ((0, 64), (1, 4)))
    q_prev = centred(keys[3], (RANK, FFN), FFN ** -0.5, 0.078125, ((1, 4),))
    return dict(acts=acts, cotangent=cotangent, error_prev=error_prev, q_prev=q_prev)


def reference(acts, cotangent, error_prev, q_prev):
    acts_rep = acts.reshape(N_DP, TOK_REP, ROWS)
    cot_rep = cotangent.reshape(N_DP, TOK_REP, FFN)
    err_rep = error_prev.reshape(N_DP, ROWS, FFN)

    def form(items):
        inputs, cots, errors = items
        gradient = lax.dot_general(inputs.astype(jnp.float32), cots.astype(jnp.float32), (((0,), (0,)), ((), ())), preferred_element_type=jnp.float32)
        return (gradient + errors.astype(jnp.float32)).astype(jnp.bfloat16)
    merged = lax.map(form, (acts_rep, cot_rep, err_rep))

    def left_part(matrix):
        return lax.dot_general(matrix.astype(jnp.float32), q_prev.astype(jnp.float32), (((1,), (1,)), ((), ())), preferred_element_type=jnp.float32)
    project = jnp.sum(lax.map(left_part, merged), axis=0)
    gram_matrix = jnp.dot(project.T.astype(jnp.float32), project.astype(jnp.float32), precision=lax.Precision.HIGHEST, preferred_element_type=jnp.float32)
    lower_factor = jnp.linalg.cholesky(gram_matrix)
    basis = jax.scipy.linalg.solve_triangular(lower_factor, project.T, lower=True).T.astype(jnp.bfloat16)

    def fold_step(carry, matrix):
        return (carry + lax.dot_general(basis.astype(jnp.float32), matrix.astype(jnp.float32), (((0,), (0,)), ((), ())), preferred_element_type=jnp.float32), None)
    q_total, _ = lax.scan(fold_step, jnp.zeros((RANK, FFN), jnp.float32), merged)
    q_new = q_total / N_DP
    low_rank = jnp.dot(basis.astype(jnp.float32), q_new.astype(jnp.bfloat16).astype(jnp.float32), preferred_element_type=jnp.float32)

    def update(matrix):
        return (matrix.astype(jnp.float32) - low_rank).astype(jnp.bfloat16)
    error_new = lax.map(update, merged).reshape(N_DP * ROWS, FFN)
    return (error_new, q_new)
```

```python
import functools

import jax
import jax.numpy as jnp
from jax import lax
from jax.experimental import pallas as pl
from jax.experimental.pallas import tpu as pltpu
from jax.sharding import PartitionSpec as P

ROWS = 1280
COLS = 1280
TOK = 1024
RANK = 64
REPLICAS = 64
NX, NY, NZ = 4, 4, 8
HALF = 640
F32 = jnp.float32
BF16 = jnp.bfloat16
ROW_CHUNKS = ((0, 256), (256, 384))
COL_CHUNKS = ((0, 256), (256, 256), (512, 256), (768, 256), (1024, 256))


def device(x, y, z, c):
    return {"dp": (y * NZ + z) * 2 + c, "tensor": x}


def send(src, dst, send_sem, recv_sem, target):
    pltpu.make_async_remote_copy(
        src_ref=src, dst_ref=dst, send_sem=send_sem, recv_sem=recv_sem,
        device_id=target, device_id_type=pl.DeviceIdType.MESH,
    ).start()


def wait_bytes(ref, sem):
    pltpu.make_async_copy(ref, ref, sem).wait()


def hops(d, n):
    return min(d, n - d)


XY = sorted(
    [(dx, dy) for dx in range(NX) for dy in range(NY) if (dx, dy) != (0, 0)],
    key=lambda d: -(hops(d[0], NX) + hops(d[1], NY)),
)
ZS = sorted(range(1, NZ), key=lambda d: -hops(d, NZ))


def slot_xy(dx, dy):
    return dx * NY + dy - 1


def eliminate(first, last, work):
    lane = lax.broadcasted_iota(jnp.int32, (RANK, 2 * RANK), 1)
    row = lax.broadcasted_iota(jnp.int32, (RANK, 2 * RANK), 0)

    def step(k, w):
        pivot_row = jnp.sum(jnp.where(row == k, w, 0.0), axis=0, keepdims=True)
        column = jnp.sum(jnp.where(lane == k, w, 0.0), axis=1, keepdims=True)
        pivot = jnp.sum(
            jnp.where(lane[:1] == k, pivot_row, 0.0), axis=1, keepdims=True
        )
        factor = column / pivot
        return w - jnp.where(row > k, factor * pivot_row, 0.0)

    return lax.fori_loop(first, last, step, work)


def sum_kernel(
    acts, cot, err, q_ref,
    merged_out, fold_out, inv_out, basis_out,
    acts_v, cot_v, err_v, q_v, at_v, merged, part,
    r1, s1, c1, u1, z1, g1, d1, proj, work,
    fb, fr, fs, z2,
    in_sem, out_sem, send_sem, recv_sem,
):
    dp = lax.axis_index("dp")
    x = lax.axis_index("tensor")
    c = lax.rem(dp, 2)
    z = lax.rem(dp // 2, NZ)
    y = dp // (2 * NZ)
    other = 1 - c

    def xy_peer(dx, dy):
        return device(lax.rem(x + dx, NX), lax.rem(y + dy, NY), z, c)

    def z_peer(dz):
        return device(x, y, lax.rem(z + dz, NZ), c)

    sibling = device(x, y, z, other)

    first_half = lax.rem(y, 2)
    loads = {}
    count = [0]

    def load(key, src, dst):
        copy = pltpu.make_async_copy(src, dst, in_sem.at[count[0]])
        count[0] += 1
        copy.start()
        loads[key] = copy

    def load_rows(s, j):
        half = lax.rem(first_half + s, 2)
        off, size = ROW_CHUNKS[j]
        start = pl.multiple_of(half * HALF + off, 128)
        load(("a", s, j), acts.at[:, pl.ds(start, size)], acts_v.at[:, pl.ds(s * HALF + off, size)])
        return start, size

    def load_err(s, j):
        half = lax.rem(first_half + s, 2)
        off, size = ROW_CHUNKS[j]
        start = pl.multiple_of(half * HALF + off, 128)
        load(("e", s, j), err.at[pl.ds(start, size), :], err_v.at[pl.ds(s * HALF + off, size), :])

    load_rows(0, 0)
    for n, (off, size) in enumerate(COL_CHUNKS):
        load(("c", n), cot.at[:, pl.ds(off, size)], cot_v.at[:, pl.ds(off, size)])
        if n == 0:
            load_err(0, 0)
    load("q", q_ref, q_v)
    load_rows(0, 1)
    load_err(0, 1)
    for j in range(2):
        load_rows(1, j)
        load_err(1, j)

    barrier = pltpu.get_barrier_semaphore()

    def greet(target):
        pl.semaphore_signal(barrier, inc=1, device_id=target, device_id_type=pl.DeviceIdType.MESH)

    for dx, dy in XY:
        greet(xy_peer(dx, dy))
    for dz in ZS:
        greet(z_peer(dz))
    greet(sibling)
    for dy in range(1, NY):
        greet(device(x, lax.rem(y + dy, NY), z, other))

    outs = []
    for s in range(2):
        half = lax.rem(first_half + s, 2)
        for j, (off, size) in enumerate(ROW_CHUNKS):
            start = pl.multiple_of(half * HALF + off, 128)
            loads[("a", s, j)].wait()
            at_v[:size, :] = acts_v[:, s * HALF + off : s * HALF + off + size].T
            if s == 0 and j == 0:
                loads[("c", 0)].wait()
            loads[("e", s, j)].wait()
            for n, (coff, csize) in enumerate(COL_CHUNKS):
                if s == 0 and j == 0 and n > 0:
                    loads[("c", n)].wait()
                grad = jnp.dot(
                    at_v[:size, :], cot_v[:, coff : coff + csize], preferred_element_type=F32
                )
                grad = grad + err_v[
                    s * HALF + off : s * HALF + off + size, coff : coff + csize
                ].astype(F32)
                merged[pl.ds(start, size), coff : coff + csize] = grad.astype(BF16)
            if s == 0 and j == 0:
                loads["q"].wait()
            part[s, :, off : off + size] = lax.dot_general(
                q_v[...], merged[pl.ds(start, size), :],
                (((1,), (1,)), ((), ())), preferred_element_type=F32,
            )
            out = pltpu.make_async_copy(
                merged.at[pl.ds(start, size), :], merged_out.at[pl.ds(start, size), :],
                out_sem.at[s * 2 + j],
            )
            out.start()
            outs.append(out)
        if s == 0:
            pl.semaphore_wait(barrier, len(XY) + len(ZS) + NY)
        for dx, dy in XY:
            if dy % 2 == s:
                tx, ty = lax.rem(x + dx, NX), lax.rem(y + dy, NY)
                block = pl.multiple_of((tx * 2 + ty // 2) * 8, 8)
                send(
                    part.at[s, pl.ds(block, 8), :], r1.at[slot_xy(dx, dy)],
                    send_sem.at[0], recv_sem.at[0], device(tx, ty, z, c),
                )

    mine = pl.multiple_of((x * 2 + y // 2) * 8, 8)
    wait_bytes(r1, recv_sem.at[0])
    total = part[0, pl.ds(mine, 8), :]
    for i in range(NX * NY - 1):
        total = total + r1[i]
    s1[...] = total
    send(s1, c1, send_sem.at[1], recv_sem.at[1], sibling)
    wait_bytes(c1, recv_sem.at[1])
    g1[...] = s1[...] + c1[...]
    own = pl.multiple_of(c * 256, 128)
    u1[...] = g1[:, pl.ds(own, 384)]
    for dz in ZS:
        send(u1, z1.at[z], send_sem.at[2], recv_sem.at[2], z_peer(dz))
    z1[z] = u1[...]
    wait_bytes(z1.at[pl.ds(0, NZ - 1)], recv_sem.at[2])
    total = z1[0]
    for i in range(1, NZ):
        total = total + z1[i]
    d1[:, pl.ds(own, 384)] = total
    give = pl.multiple_of(c * 384, 128)
    send(
        d1.at[:, pl.ds(give, 256)], d1.at[:, pl.ds(give, 256)],
        send_sem.at[3], recv_sem.at[3], sibling,
    )
    wait_bytes(d1.at[:, pl.ds(0, 256)], recv_sem.at[3])
    lanes = pl.ds(pl.multiple_of(lax.rem(y, 2) * HALF, 128), HALF)
    home = proj.at[pl.ds(mine, 8), lanes]
    for dx, dy in XY:
        send(d1, home, send_sem.at[4], recv_sem.at[4], xy_peer(dx, dy))
    proj[pl.ds(mine, 8), lanes] = d1[...]
    wait_bytes(r1, recv_sem.at[4])

    left = proj[...]
    high = left.astype(BF16)
    low = (left - high.astype(F32)).astype(BF16)
    stack = jnp.concatenate([high, low], axis=0)
    for h in range(2):
        both = jnp.dot(stack, merged[:, h * HALF : (h + 1) * HALF], preferred_element_type=F32)
        fb[:, h * HALF : (h + 1) * HALF] = (both[:RANK] + both[RANK:]).astype(BF16)
        for dy in (2, 1, 3, 0):
            ty = lax.rem(y + dy, NY)
            rows = pl.ds(pl.multiple_of(ty * 16, 16), 16)

            def give_fold():
                send(
                    fb.at[rows, pl.ds(h * HALF, HALF)], fr.at[y * 2 + c],
                    send_sem.at[5], recv_sem.at[5], device(x, ty, z, h),
                )

            if dy:
                give_fold()
            else:
                pl.when(c != h)(give_fold)
    fr[y * 2 + c] = fb[
        pl.ds(pl.multiple_of(y * 16, 16), 16), pl.ds(pl.multiple_of(c * HALF, 128), HALF)
    ]

    gram = lax.dot_general(
        left, left, (((1,), (1,)), ((), ())),
        precision=lax.Precision.HIGHEST, preferred_element_type=F32,
    )
    eye = (
        lax.broadcasted_iota(jnp.int32, (RANK, RANK), 0)
        == lax.broadcasted_iota(jnp.int32, (RANK, RANK), 1)
    ).astype(F32)
    work[...] = eliminate(0, 20, jnp.concatenate([gram, eye], axis=1))

    wait_bytes(fr.at[pl.ds(0, 2 * NY - 1)], recv_sem.at[5])
    total = fr[0].astype(F32)
    for i in range(1, 2 * NY):
        total = total + fr[i].astype(F32)
    z2[z] = total.astype(BF16)
    for dz in ZS:
        send(z2.at[z], z2.at[z], send_sem.at[6], recv_sem.at[6], z_peer(dz))
    work[...] = eliminate(20, RANK, work[...])
    wait_bytes(z2.at[pl.ds(0, NZ - 1)], recv_sem.at[6])
    total = z2[0].astype(F32)
    for i in range(1, NZ):
        total = total + z2[i].astype(F32)
    rows = pl.ds(pl.multiple_of(y * 16, 16), 16)
    lanes = pl.ds(pl.multiple_of(c * HALF, 128), HALF)
    fs[rows, lanes] = total.astype(BF16)
    for dy in (2, 1, 3):
        ty = lax.rem(y + dy, NY)
        for core in (other, c):
            send(
                fs.at[rows, lanes], fs.at[rows, lanes],
                send_sem.at[7], recv_sem.at[7], device(x, ty, z, core),
            )
    send(fs.at[rows, lanes], fs.at[rows, lanes], send_sem.at[7], recv_sem.at[7], sibling)

    eliminated = work[...]
    diagonal = jnp.sum(eliminated[:, :RANK] * eye, axis=1, keepdims=True)
    inverse = eliminated[:, RANK:] * lax.rsqrt(diagonal)
    inv_out[...] = inverse
    basis_out[...] = jnp.dot(
        inverse, proj[...], precision=lax.Precision.HIGHEST, preferred_element_type=F32
    ).astype(BF16)

    wait_bytes(fr.at[pl.ds(0, 2 * NY - 1)], recv_sem.at[7])
    fold_out[...] = fs[...]

    wait_bytes(r1, send_sem.at[0])
    wait_bytes(s1, send_sem.at[1])
    wait_bytes(z1.at[pl.ds(0, NZ - 1)], send_sem.at[2])
    wait_bytes(d1.at[:, pl.ds(0, 256)], send_sem.at[3])
    wait_bytes(r1, send_sem.at[4])
    wait_bytes(fr.at[pl.ds(0, 2 * NY - 1)], send_sem.at[5])
    wait_bytes(z2.at[pl.ds(0, NZ - 1)], send_sem.at[6])
    wait_bytes(fr.at[pl.ds(0, 2 * NY - 1)], send_sem.at[7])
    for out in outs:
        out.wait()


def update_kernel(merged, fold, inv, basis, error_new, q_new, q_low):
    @pl.when(pl.program_id(0) == 0)
    def _():
        q = jnp.dot(
            inv[...], fold[...].astype(F32),
            precision=lax.Precision.HIGHEST, preferred_element_type=F32,
        ) * (1.0 / REPLICAS)
        q_new[...] = q
        q_low[...] = q.astype(BF16)

    low_rank = lax.dot_general(
        basis[...], q_low[...], (((0,), (0,)), ((), ())), preferred_element_type=F32
    )
    error_new[...] = (merged[...].astype(F32) - low_rank).astype(BF16)


def body(acts, cotangent, error_prev, q_prev):
    anywhere = pl.BlockSpec(memory_space=pl.ANY)
    inside = pl.BlockSpec(memory_space=pltpu.VMEM)
    merged, fold, inv, basis = pl.pallas_call(
        sum_kernel,
        out_shape=(
            jax.ShapeDtypeStruct((ROWS, COLS), BF16),
            jax.ShapeDtypeStruct((RANK, COLS), BF16),
            jax.ShapeDtypeStruct((RANK, RANK), F32),
            jax.ShapeDtypeStruct((RANK, ROWS), BF16),
        ),
        in_specs=[anywhere] * 4,
        out_specs=(anywhere, inside, inside, inside),
        scratch_shapes=[
            pltpu.VMEM((TOK, ROWS), BF16),
            pltpu.VMEM((TOK, COLS), BF16),
            pltpu.VMEM((ROWS, COLS), BF16),
            pltpu.VMEM((RANK, COLS), BF16),
            pltpu.VMEM((384, TOK), BF16),
            pltpu.VMEM((ROWS, COLS), BF16),
            pltpu.VMEM((2, RANK, HALF), F32),
            pltpu.VMEM((NX * NY - 1, 8, HALF), F32),
            pltpu.VMEM((8, HALF), F32),
            pltpu.VMEM((8, HALF), F32),
            pltpu.VMEM((8, 384), F32),
            pltpu.VMEM((NZ, 8, 384), F32),
            pltpu.VMEM((8, HALF), F32),
            pltpu.VMEM((8, HALF), F32),
            pltpu.VMEM((RANK, ROWS), F32),
            pltpu.VMEM((RANK, 2 * RANK), F32),
            pltpu.VMEM((RANK, COLS), BF16),
            pltpu.VMEM((2 * NY, 16, HALF), BF16),
            pltpu.VMEM((RANK, COLS), BF16),
            pltpu.VMEM((NZ, 16, HALF), BF16),
            pltpu.SemaphoreType.DMA((14,)),
            pltpu.SemaphoreType.DMA((4,)),
            pltpu.SemaphoreType.DMA((8,)),
            pltpu.SemaphoreType.DMA((8,)),
        ],
        compiler_params=pltpu.CompilerParams(
            collective_id=0, has_side_effects=True, vmem_limit_bytes=56 << 20
        ),
        name="sums",
    )(acts, cotangent, error_prev, q_prev)

    block = 256
    whole = lambda shape: pl.BlockSpec(shape, lambda i: (0, 0))
    error_new, q_new = pl.pallas_call(
        update_kernel,
        grid=(ROWS // block,),
        in_specs=[
            pl.BlockSpec((block, COLS), lambda i: (i, 0)),
            whole((RANK, COLS)),
            whole((RANK, RANK)),
            pl.BlockSpec((RANK, block), lambda i: (0, i)),
        ],
        out_specs=(pl.BlockSpec((block, COLS), lambda i: (i, 0)), whole((RANK, COLS))),
        out_shape=(
            jax.ShapeDtypeStruct((ROWS, COLS), BF16),
            jax.ShapeDtypeStruct((RANK, COLS), F32),
        ),
        scratch_shapes=[pltpu.VMEM((RANK, COLS), BF16)],
        compiler_params=pltpu.CompilerParams(vmem_limit_bytes=40 << 20),
        name="update",
    )(merged, fold, inv, basis)
    return error_new, q_new


def solution(mesh):
    return jax.shard_map(
        body,
        mesh=mesh,
        in_specs=(P("dp", None), P("dp", "tensor"), P("dp", "tensor"), P(None, "tensor")),
        out_specs=(P("dp", "tensor"), P(None, "tensor")),
        check_vma=False,
    )
```

```python
import functools

import jax
import jax.numpy as jnp
from jax import lax
from jax.experimental import pallas as pl
from jax.experimental.pallas import tpu as pltpu
from jax.sharding import PartitionSpec as P

ROWS = 1280
COLS = 1280
TOK = 1024
RANK = 64
REPLICAS = 64
NX, NY, NZ = 4, 4, 8
HALF = 640
F32 = jnp.float32
BF16 = jnp.bfloat16
STEP = 256


def device(x, y, z, c):
    return {"dp": (y * NZ + z) * 2 + c, "tensor": x}


def send(src, dst, send_sem, recv_sem, target):
    pltpu.make_async_remote_copy(
        src_ref=src, dst_ref=dst, send_sem=send_sem, recv_sem=recv_sem,
        device_id=target, device_id_type=pl.DeviceIdType.MESH,
    ).start()


def wait_bytes(ref, sem):
    pltpu.make_async_copy(ref, ref, sem).wait()


def hops(d, n):
    return min(d, n - d)


XY = sorted(
    [(dx, dy) for dx in range(NX) for dy in range(NY) if (dx, dy) != (0, 0)],
    key=lambda d: -(hops(d[0], NX) + hops(d[1], NY)),
)
ZS = sorted(range(1, NZ), key=lambda d: -hops(d, NZ))


def slot_xy(dx, dy):
    return dx * NY + dy - 1


def eliminate(first, last, work):
    lane = lax.broadcasted_iota(jnp.int32, (RANK, 2 * RANK), 1)
    row = lax.broadcasted_iota(jnp.int32, (RANK, 2 * RANK), 0)

    def step(k, w):
        pivot_row = jnp.sum(jnp.where(row == k, w, 0.0), axis=0, keepdims=True)
        column = jnp.sum(jnp.where(lane == k, w, 0.0), axis=1, keepdims=True)
        pivot = jnp.sum(
            jnp.where(lane[:1] == k, pivot_row, 0.0), axis=1, keepdims=True
        )
        factor = column / pivot
        return w - jnp.where(row > k, factor * pivot_row, 0.0)

    return lax.fori_loop(first, last, step, work)


def sum_kernel(
    acts, cot, err, q_ref,
    merged, q_new, q_low, basis_out,
    acts_v, cot_v, err_v, q_v, weight, part,
    r1, s1, c1, u1, z1, g1, d1, proj, work,
    fb, fr, fs, z2,
    in_sem, send_sem, recv_sem,
):
    dp = lax.axis_index("dp")
    x = lax.axis_index("tensor")
    c = lax.rem(dp, 2)
    z = lax.rem(dp // 2, NZ)
    y = dp // (2 * NZ)
    other = 1 - c

    def xy_peer(dx, dy):
        return device(lax.rem(x + dx, NX), lax.rem(y + dy, NY), z, c)

    def z_peer(dz):
        return device(x, y, lax.rem(z + dz, NZ), c)

    sibling = device(x, y, z, other)

    copies = [pltpu.make_async_copy(q_ref, q_v, in_sem.at[0])]

    def plan(src, dst, rows, step):
        for r in range(0, rows, step):
            block = pl.ds(r, step)
            copies.append(
                pltpu.make_async_copy(src.at[block], dst.at[block], in_sem.at[len(copies)])
            )

    plan(cot, cot_v, TOK, 512)
    plan(err, err_v, ROWS, STEP)
    plan(acts, acts_v, TOK, STEP)
    turn = [0, 0]

    def start_copies(upto):
        while turn[0] < min(upto, len(copies)):
            copies[turn[0]].start()
            turn[0] += 1

    def next_copy():
        copies[turn[1]].wait()
        turn[1] += 1
        start_copies(turn[1] + 3)

    start_copies(4)
    barrier = pltpu.get_barrier_semaphore()

    def greet(target):
        pl.semaphore_signal(barrier, inc=1, device_id=target, device_id_type=pl.DeviceIdType.MESH)

    for dx, dy in XY:
        greet(xy_peer(dx, dy))
    for dz in ZS:
        greet(z_peer(dz))
    greet(sibling)
    for dy in range(1, NY):
        greet(device(x, lax.rem(y + dy, NY), z, other))

    next_copy()
    for r in range(0, TOK, 512):
        next_copy()
        product = lax.dot_general(
            cot_v[r : r + 512, :], q_v[...], (((1,), (1,)), ((), ())), preferred_element_type=F32
        )
        high = product.astype(BF16)
        low = (product - high.astype(F32)).astype(BF16)
        weight[r : r + 512, :] = jnp.concatenate([high, low], axis=1)
    for r in range(0, ROWS, STEP):
        next_copy()
        part[:, r : r + STEP] = lax.dot_general(
            q_v[...], err_v[r : r + STEP, :], (((1,), (1,)), ((), ())),
            preferred_element_type=F32,
        )
    for r in range(0, TOK, STEP):
        next_copy()
        both = lax.dot_general(
            weight[r : r + STEP, :], acts_v[r : r + STEP, :], (((0,), (0,)), ((), ())),
            preferred_element_type=F32,
        )
        part[...] += both[:RANK] + both[RANK:]
    pl.semaphore_wait(barrier, len(XY) + len(ZS) + NY)
    for dx, dy in XY:
        tx, ty = lax.rem(x + dx, NX), lax.rem(y + dy, NY)
        block = pl.multiple_of((tx * 2 + ty // 2) * 8, 8)
        lanes = pl.ds(pl.multiple_of(lax.rem(ty, 2) * HALF, 128), HALF)
        send(
            part.at[pl.ds(block, 8), lanes], r1.at[slot_xy(dx, dy)],
            send_sem.at[0], recv_sem.at[0], device(tx, ty, z, c),
        )

    for r in range(0, ROWS, STEP):
        grad = lax.dot_general(
            acts_v[:, r : r + STEP], cot_v[...], (((0,), (0,)), ((), ())),
            preferred_element_type=F32,
        )
        merged[r : r + STEP, :] = (grad + err_v[r : r + STEP, :].astype(F32)).astype(BF16)

    mine = pl.multiple_of((x * 2 + y // 2) * 8, 8)
    wait_bytes(r1, recv_sem.at[0])
    lanes = pl.ds(pl.multiple_of(lax.rem(y, 2) * HALF, 128), HALF)
    total = part[pl.ds(mine, 8), lanes]
    for i in range(NX * NY - 1):
        total = total + r1[i]
    s1[...] = total
    send(s1, c1, send_sem.at[1], recv_sem.at[1], sibling)
    wait_bytes(c1, recv_sem.at[1])
    g1[...] = s1[...] + c1[...]
    own = pl.multiple_of(c * 256, 128)
    u1[...] = g1[:, pl.ds(own, 384)]
    for dz in ZS:
        send(u1, z1.at[z], send_sem.at[2], recv_sem.at[2], z_peer(dz))
    z1[z] = u1[...]
    wait_bytes(z1.at[pl.ds(0, NZ - 1)], recv_sem.at[2])
    total = z1[0]
    for i in range(1, NZ):
        total = total + z1[i]
    d1[:, pl.ds(own, 384)] = total
    give = pl.multiple_of(c * 384, 128)
    send(
        d1.at[:, pl.ds(give, 256)], d1.at[:, pl.ds(give, 256)],
        send_sem.at[3], recv_sem.at[3], sibling,
    )
    wait_bytes(d1.at[:, pl.ds(0, 256)], recv_sem.at[3])
    home = proj.at[pl.ds(mine, 8), lanes]
    for dx, dy in XY:
        send(d1, home, send_sem.at[4], recv_sem.at[4], xy_peer(dx, dy))
    proj[pl.ds(mine, 8), lanes] = d1[...]
    wait_bytes(r1, recv_sem.at[4])

    left = proj[...]
    high = left.astype(BF16)
    low = (left - high.astype(F32)).astype(BF16)
    stack = jnp.concatenate([high, low], axis=0)
    for h in range(2):
        both = jnp.dot(stack, merged[:, h * HALF : (h + 1) * HALF], preferred_element_type=F32)
        fb[:, h * HALF : (h + 1) * HALF] = (both[:RANK] + both[RANK:]).astype(BF16)
        for dy in (2, 1, 3, 0):
            ty = lax.rem(y + dy, NY)
            rows = pl.ds(pl.multiple_of(ty * 16, 16), 16)

            def give_fold():
                send(
                    fb.at[rows, pl.ds(h * HALF, HALF)], fr.at[y * 2 + c],
                    send_sem.at[5], recv_sem.at[5], device(x, ty, z, h),
                )

            if dy:
                give_fold()
            else:
                pl.when(c != h)(give_fold)
    fr[y * 2 + c] = fb[
        pl.ds(pl.multiple_of(y * 16, 16), 16), pl.ds(pl.multiple_of(c * HALF, 128), HALF)
    ]

    gram = lax.dot_general(
        left, left, (((1,), (1,)), ((), ())),
        precision=lax.Precision.HIGHEST, preferred_element_type=F32,
    )
    eye = (
        lax.broadcasted_iota(jnp.int32, (RANK, RANK), 0)
        == lax.broadcasted_iota(jnp.int32, (RANK, RANK), 1)
    ).astype(F32)
    work[...] = eliminate(0, 20, jnp.concatenate([gram, eye], axis=1))

    wait_bytes(fr.at[pl.ds(0, 2 * NY - 1)], recv_sem.at[5])
    total = fr[0].astype(F32)
    for i in range(1, 2 * NY):
        total = total + fr[i].astype(F32)
    z2[z] = total.astype(BF16)
    for dz in ZS:
        send(z2.at[z], z2.at[z], send_sem.at[6], recv_sem.at[6], z_peer(dz))
    work[...] = eliminate(20, RANK, work[...])
    wait_bytes(z2.at[pl.ds(0, NZ - 1)], recv_sem.at[6])
    total = z2[0].astype(F32)
    for i in range(1, NZ):
        total = total + z2[i].astype(F32)
    rows = pl.ds(pl.multiple_of(y * 16, 16), 16)
    lanes = pl.ds(pl.multiple_of(c * HALF, 128), HALF)
    fs[rows, lanes] = total.astype(BF16)
    for dy in (2, 1, 3):
        ty = lax.rem(y + dy, NY)
        for core in (other, c):
            send(
                fs.at[rows, lanes], fs.at[rows, lanes],
                send_sem.at[7], recv_sem.at[7], device(x, ty, z, core),
            )
    send(fs.at[rows, lanes], fs.at[rows, lanes], send_sem.at[7], recv_sem.at[7], sibling)

    eliminated = work[...]
    diagonal = jnp.sum(eliminated[:, :RANK] * eye, axis=1, keepdims=True)
    inverse = eliminated[:, RANK:] * lax.rsqrt(diagonal)
    basis_out[...] = jnp.dot(
        inverse, proj[...], precision=lax.Precision.HIGHEST, preferred_element_type=F32
    ).astype(BF16)

    wait_bytes(fr.at[pl.ds(0, 2 * NY - 1)], recv_sem.at[7])
    q = jnp.dot(
        inverse, fs[...].astype(F32), precision=lax.Precision.HIGHEST, preferred_element_type=F32
    ) * (1.0 / REPLICAS)
    q_new[...] = q
    q_low[...] = q.astype(BF16)


    wait_bytes(r1, send_sem.at[0])
    wait_bytes(s1, send_sem.at[1])
    wait_bytes(z1.at[pl.ds(0, NZ - 1)], send_sem.at[2])
    wait_bytes(d1.at[:, pl.ds(0, 256)], send_sem.at[3])
    wait_bytes(r1, send_sem.at[4])
    wait_bytes(fr.at[pl.ds(0, 2 * NY - 1)], send_sem.at[5])
    wait_bytes(z2.at[pl.ds(0, NZ - 1)], send_sem.at[6])
    wait_bytes(fr.at[pl.ds(0, 2 * NY - 1)], send_sem.at[7])


def update_kernel(merged, q_in, q_low, basis, error_new, q_new, error_v, sem):
    copies = [pltpu.make_async_copy(q_in, q_new, sem.at[0])]
    copies[0].start()
    for r in range(0, ROWS, STEP):
        low_rank = lax.dot_general(
            basis[:, r : r + STEP], q_low[...], (((0,), (0,)), ((), ())),
            preferred_element_type=F32,
        )
        error_v[r : r + STEP, :] = (merged[r : r + STEP, :].astype(F32) - low_rank).astype(BF16)
        block = pl.ds(r, STEP)
        copies.append(
            pltpu.make_async_copy(error_v.at[block], error_new.at[block], sem.at[len(copies)])
        )
        copies[-1].start()
    for copy in copies:
        copy.wait()


def body(acts, cotangent, error_prev, q_prev):
    anywhere = pl.BlockSpec(memory_space=pl.ANY)
    inside = pl.BlockSpec(memory_space=pltpu.VMEM)
    outside = [
        pltpu.with_memory_space_constraint(a, pltpu.HBM)
        for a in (acts, cotangent, error_prev, q_prev)
    ]
    results = pl.pallas_call(
        sum_kernel,
        out_shape=(
            pltpu.VMEM((ROWS, COLS), BF16),
            pltpu.VMEM((RANK, COLS), F32),
            pltpu.VMEM((RANK, COLS), BF16),
            pltpu.VMEM((RANK, ROWS), BF16),
        ),
        in_specs=[anywhere] * 4,
        out_specs=(inside,) * 4,
        scratch_shapes=[
            pltpu.VMEM((TOK, ROWS), BF16),
            pltpu.VMEM((TOK, COLS), BF16),
            pltpu.VMEM((ROWS, COLS), BF16),
            pltpu.VMEM((RANK, COLS), BF16),
            pltpu.VMEM((TOK, 2 * RANK), BF16),
            pltpu.VMEM((RANK, ROWS), F32),
            pltpu.VMEM((NX * NY - 1, 8, HALF), F32),
            pltpu.VMEM((8, HALF), F32),
            pltpu.VMEM((8, HALF), F32),
            pltpu.VMEM((8, 384), F32),
            pltpu.VMEM((NZ, 8, 384), F32),
            pltpu.VMEM((8, HALF), F32),
            pltpu.VMEM((8, HALF), F32),
            pltpu.VMEM((RANK, ROWS), F32),
            pltpu.VMEM((RANK, 2 * RANK), F32),
            pltpu.VMEM((RANK, COLS), BF16),
            pltpu.VMEM((2 * NY, 16, HALF), BF16),
            pltpu.VMEM((RANK, COLS), BF16),
            pltpu.VMEM((NZ, 16, HALF), BF16),
            pltpu.SemaphoreType.DMA((12,)),
            pltpu.SemaphoreType.DMA((8,)),
            pltpu.SemaphoreType.DMA((8,)),
        ],
        compiler_params=pltpu.CompilerParams(
            collective_id=0, has_side_effects=True, vmem_limit_bytes=40 << 20
        ),
        name="sums",
    )(*outside)
    results = [pltpu.with_memory_space_constraint(a, pltpu.VMEM) for a in results]
    return pl.pallas_call(
        update_kernel,
        in_specs=[inside] * 4,
        out_specs=(anywhere, anywhere),
        out_shape=(
            jax.ShapeDtypeStruct((ROWS, COLS), BF16),
            jax.ShapeDtypeStruct((RANK, COLS), F32),
        ),
        scratch_shapes=[
            pltpu.VMEM((ROWS, COLS), BF16),
            pltpu.SemaphoreType.DMA((1 + ROWS // STEP,)),
        ],
        compiler_params=pltpu.CompilerParams(vmem_limit_bytes=40 << 20),
        name="update",
    )(*results)


def solution(mesh):
    return jax.shard_map(
        body,
        mesh=mesh,
        in_specs=(P("dp", None), P("dp", "tensor"), P("dp", "tensor"), P(None, "tensor")),
        out_specs=(P("dp", "tensor"), P(None, "tensor")),
        check_vma=False,
    )
```

```python
import functools

import jax
import jax.numpy as jnp
from jax import lax
from jax.experimental import pallas as pl
from jax.experimental.pallas import tpu as pltpu
from jax.sharding import PartitionSpec as P

ROWS = 1280
COLS = 1280
TOK = 1024
RANK = 64
REPLICAS = 64
NX, NY, NZ = 4, 4, 8
HALF = 640
WIDE = 384
F32 = jnp.float32
BF16 = jnp.bfloat16
STEP = 256


def device(x, y, z, c):
    return {"dp": (y * NZ + z) * 2 + c, "tensor": x}


def send(src, dst, send_sem, recv_sem, target):
    pltpu.make_async_remote_copy(
        src_ref=src, dst_ref=dst, send_sem=send_sem, recv_sem=recv_sem,
        device_id=target, device_id_type=pl.DeviceIdType.MESH,
    ).start()


def wait_bytes(ref, sem):
    pltpu.make_async_copy(ref, ref, sem).wait()


def hops(d, n):
    return min(d, n - d)


XY = sorted(
    [(dx, dy) for dx in range(NX) for dy in range(NY) if (dx, dy) != (0, 0)],
    key=lambda d: -(hops(d[0], NX) + hops(d[1], NY)),
)
ZS = sorted(range(1, NZ), key=lambda d: -hops(d, NZ))


def ranks(i):
    return pl.ds(pl.multiple_of(i * 8, 8), 8)


def lanes(j):
    return pl.ds(pl.multiple_of(j * 256 + j // 2 * 128, 128), WIDE)


def sixteen(i):
    return pl.ds(pl.multiple_of(i * 16, 16), 16)


def lane_half(i):
    return pl.ds(pl.multiple_of(i * HALF, 128), HALF)


def slot_xy(dx, dy):
    return dx * NY + dy - 1


def eliminate(first, last, work):
    lane = lax.broadcasted_iota(jnp.int32, (RANK, 2 * RANK), 1)
    row = lax.broadcasted_iota(jnp.int32, (RANK, 2 * RANK), 0)

    def step(k, w):
        pivot_row = jnp.sum(jnp.where(row == k, w, 0.0), axis=0, keepdims=True)
        column = jnp.sum(jnp.where(lane == k, w, 0.0), axis=1, keepdims=True)
        pivot = jnp.sum(
            jnp.where(lane[:1] == k, pivot_row, 0.0), axis=1, keepdims=True
        )
        factor = column / pivot
        return w - jnp.where(row > k, factor * pivot_row, 0.0)

    return lax.fori_loop(first, last, step, work)


def sum_kernel(
    acts, cot, err, q_ref,
    merged, q_new, q_low, basis_out,
    acts_v, cot_v, err_v, q_v, weight, part,
    c0, half, twin, r1, z1, g1, proj, work,
    fb, fr, fs, z2,
    in_sem, core_send, core_recv, send_sem, recv_sem,
):
    dp = lax.axis_index("dp")
    x = lax.axis_index("tensor")
    c = lax.rem(dp, 2)
    z = lax.rem(dp // 2, NZ)
    y = dp // (2 * NZ)
    other = 1 - c

    def xy_peer(dx, dy):
        return device(lax.rem(x + dx, NX), lax.rem(y + dy, NY), z, c)

    def z_peer(dz):
        return device(x, y, lax.rem(z + dz, NZ), c)

    sibling = device(x, y, z, other)

    copies = [pltpu.make_async_copy(q_ref, q_v, in_sem.at[0])]

    def plan(pairs):
        for src, dst in pairs:
            copies.append(pltpu.make_async_copy(src, dst, in_sem.at[len(copies)]))

    plan([(cot.at[pl.ds(r, 512)], cot_v.at[pl.ds(r, 512)]) for r in range(0, TOK, 512)])
    plan([(err, err_v), (acts, acts_v)])
    turn = [0, 0]

    def start_copies(upto):
        while turn[0] < min(upto, len(copies)):
            copies[turn[0]].start()
            turn[0] += 1

    def next_copy():
        copies[turn[1]].wait()
        turn[1] += 1
        start_copies(turn[1] + 3)

    start_copies(4)
    barrier = pltpu.get_barrier_semaphore()

    def greet(target):
        pl.semaphore_signal(barrier, inc=1, device_id=target, device_id_type=pl.DeviceIdType.MESH)

    for dx, dy in XY:
        greet(xy_peer(dx, dy))
    for dz in ZS:
        greet(z_peer(dz))
    greet(sibling)
    for dy in range(1, NY):
        greet(device(x, lax.rem(y + dy, NY), z, other))

    next_copy()
    for r in range(0, TOK, 512):
        next_copy()
        product = lax.dot_general(
            cot_v[r : r + 512, :], q_v[...], (((1,), (1,)), ((), ())), preferred_element_type=F32
        )
        high = product.astype(BF16)
        low = (product - high.astype(F32)).astype(BF16)
        weight[r : r + 512, :] = jnp.concatenate([high, low], axis=1)
    next_copy()
    for r in range(0, ROWS, STEP):
        part[:, r : r + STEP] = lax.dot_general(
            q_v[...], err_v[r : r + STEP, :], (((1,), (1,)), ((), ())),
            preferred_element_type=F32,
        )
    ours = pl.ds(pl.multiple_of(c * 32, 32), 32)
    theirs = pl.ds(pl.multiple_of(other * 32, 32), 32)
    next_copy()
    for i, r in enumerate(range(0, ROWS, STEP)):
        both = lax.dot_general(
            weight[...], acts_v[:, r : r + STEP], (((0,), (0,)), ((), ())),
            preferred_element_type=F32,
        )
        part[:, r : r + STEP] += both[:RANK] + both[RANK:]
        if i == 0:
            pl.semaphore_wait(barrier, len(XY) + len(ZS) + NY)
        columns = pl.ds(r, STEP)
        send(
            part.at[theirs, columns], c0.at[:, columns], core_send.at[i], core_recv.at[i], sibling
        )
    for i, r in enumerate(range(0, ROWS, STEP)):
        columns = pl.ds(r, STEP)
        wait_bytes(c0.at[:, columns], core_recv.at[i])
        half[:, columns] = part[ours, columns] + c0[:, columns]
    for dx, dy in XY:
        tx, ty = lax.rem(x + dx, NX), lax.rem(y + dy, NY)
        send(
            half.at[ranks(tx), lanes(ty)], r1.at[slot_xy(dx, dy)],
            send_sem.at[0], recv_sem.at[0], device(tx, ty, z, c),
        )

    for r in range(0, ROWS, STEP):
        grad = lax.dot_general(
            acts_v[:, r : r + STEP], cot_v[...], (((0,), (0,)), ((), ())),
            preferred_element_type=F32,
        )
        merged[r : r + STEP, :] = (grad + err_v[r : r + STEP, :].astype(F32)).astype(BF16)
        block = pl.ds(r, STEP)
        send(merged.at[block], twin.at[block], send_sem.at[4], recv_sem.at[4], sibling)

    wait_bytes(r1, recv_sem.at[0])
    total = half[ranks(x), lanes(y)]
    for i in range(NX * NY - 1):
        total = total + r1[i]
    z1[z] = total
    for dz in ZS:
        send(z1.at[z], z1.at[z], send_sem.at[1], recv_sem.at[1], z_peer(dz))
    wait_bytes(z1.at[pl.ds(0, NZ - 1)], recv_sem.at[1])
    total = z1[0]
    for i in range(1, NZ):
        total = total + z1[i]
    mine = x * NY + y
    g1[mine] = total
    for dx, dy in XY:
        send(g1.at[mine], g1.at[mine], send_sem.at[2], recv_sem.at[2], xy_peer(dx, dy))
    wait_bytes(r1, recv_sem.at[2])
    for i in range(NX):
        for j in range(NY):
            start = j * 256 + j // 2 * 128
            c0[8 * i : 8 * i + 8, start : start + WIDE] = g1[i * NY + j]
    send(c0, proj.at[ours], send_sem.at[3], recv_sem.at[3], sibling)
    wait_bytes(twin, recv_sem.at[4])
    left = c0[...]
    high = left.astype(BF16)
    low = (left - high.astype(F32)).astype(BF16)
    stack = jnp.concatenate([high, low], axis=0)
    for h in range(2):
        columns = pl.ds(h * HALF, HALF)
        both = jnp.dot(stack, merged[:, columns], preferred_element_type=F32)
        both = both + jnp.dot(stack, twin[:, columns], preferred_element_type=F32)
        fb[:, columns] = (both[:32] + both[32:]).astype(BF16)
        for dy in (2, 1, 3):
            ty = lax.rem(y + dy, NY)

            @pl.when(lax.rem(ty, 2) == h)
            def _():
                send(
                    fb.at[sixteen(ty // 2), columns], fr.at[y],
                    send_sem.at[5], recv_sem.at[5], device(x, ty, z, c),
                )

    fr[y] = fb[sixteen(y // 2), lane_half(lax.rem(y, 2))]

    proj[ours, :] = left
    wait_bytes(half, recv_sem.at[3])
    left = proj[...]
    gram = lax.dot_general(
        left, left, (((1,), (1,)), ((), ())),
        precision=lax.Precision.HIGHEST, preferred_element_type=F32,
    )
    eye = (
        lax.broadcasted_iota(jnp.int32, (RANK, RANK), 0)
        == lax.broadcasted_iota(jnp.int32, (RANK, RANK), 1)
    ).astype(F32)
    work[...] = eliminate(0, 12, jnp.concatenate([gram, eye], axis=1))

    wait_bytes(fr.at[pl.ds(0, NY - 1)], recv_sem.at[5])
    total = fr[0].astype(F32)
    for i in range(1, NY):
        total = total + fr[i].astype(F32)
    z2[z] = total.astype(BF16)
    for dz in ZS:
        send(z2.at[z], z2.at[z], send_sem.at[6], recv_sem.at[6], z_peer(dz))
    work[...] = eliminate(12, 46, work[...])
    wait_bytes(z2.at[pl.ds(0, NZ - 1)], recv_sem.at[6])
    total = z2[0].astype(F32)
    for i in range(1, NZ):
        total = total + z2[i].astype(F32)
    here = fs.at[sixteen(2 * c + y // 2), lane_half(lax.rem(y, 2))]
    landed = z2.at[pl.ds(0, NZ - 1)]
    here[...] = total.astype(BF16)
    for dy in (2, 1, 3):
        ty = lax.rem(y + dy, NY)
        for core in (other, c):
            send(
                here, here,
                send_sem.at[7], recv_sem.at[7], device(x, ty, z, core),
            )
    send(here, here, send_sem.at[7], recv_sem.at[7], sibling)

    eliminated = eliminate(46, RANK, work[...])
    diagonal = jnp.sum(eliminated[:, :RANK] * eye, axis=1, keepdims=True)
    inverse = eliminated[:, RANK:] * lax.rsqrt(diagonal)
    basis_out[...] = jnp.dot(
        inverse, proj[...], precision=lax.Precision.HIGHEST, preferred_element_type=F32
    ).astype(BF16)

    wait_bytes(landed, recv_sem.at[7])
    high = inverse.astype(BF16)
    low = (inverse - high.astype(F32)).astype(BF16)
    both = jnp.dot(
        jnp.concatenate([high, low], axis=0), fs[...], preferred_element_type=F32
    )
    q = (both[:RANK] + both[RANK:]) * (1.0 / REPLICAS)
    q_new[...] = q
    q_low[...] = q.astype(BF16)


    for i, r in enumerate(range(0, ROWS, STEP)):
        wait_bytes(c0.at[:, pl.ds(r, STEP)], core_send.at[i])
    wait_bytes(r1, send_sem.at[0])
    wait_bytes(z1.at[pl.ds(0, NZ - 1)], send_sem.at[1])
    wait_bytes(r1, send_sem.at[2])
    wait_bytes(half, send_sem.at[3])
    wait_bytes(twin, send_sem.at[4])
    wait_bytes(fr.at[pl.ds(0, NY - 1)], send_sem.at[5])
    wait_bytes(z2.at[pl.ds(0, NZ - 1)], send_sem.at[6])
    wait_bytes(landed, send_sem.at[7])


def update_kernel(merged, q_in, q_low, basis, error_new, q_new, error_v, sem):
    copies = [pltpu.make_async_copy(q_in, q_new, sem.at[0])]
    copies[0].start()
    for r in range(0, ROWS, STEP):
        low_rank = lax.dot_general(
            basis[:, r : r + STEP], q_low[...], (((0,), (0,)), ((), ())),
            preferred_element_type=F32,
        )
        error_v[r : r + STEP, :] = (merged[r : r + STEP, :].astype(F32) - low_rank).astype(BF16)
        block = pl.ds(r, STEP)
        copies.append(
            pltpu.make_async_copy(error_v.at[block], error_new.at[block], sem.at[len(copies)])
        )
        copies[-1].start()
    for copy in copies:
        copy.wait()


def body(acts, cotangent, error_prev, q_prev):
    anywhere = pl.BlockSpec(memory_space=pl.ANY)
    inside = pl.BlockSpec(memory_space=pltpu.VMEM)
    outside = [
        pltpu.with_memory_space_constraint(a, pltpu.HBM)
        for a in (acts, cotangent, error_prev, q_prev)
    ]
    results = pl.pallas_call(
        sum_kernel,
        out_shape=(
            pltpu.VMEM((ROWS, COLS), BF16),
            pltpu.VMEM((RANK, COLS), F32),
            pltpu.VMEM((RANK, COLS), BF16),
            pltpu.VMEM((RANK, ROWS), BF16),
        ),
        in_specs=[anywhere] * 4,
        out_specs=(inside,) * 4,
        scratch_shapes=[
            pltpu.VMEM((TOK, ROWS), BF16),
            pltpu.VMEM((TOK, COLS), BF16),
            pltpu.VMEM((ROWS, COLS), BF16),
            pltpu.VMEM((RANK, COLS), BF16),
            pltpu.VMEM((TOK, 2 * RANK), BF16),
            pltpu.VMEM((RANK, ROWS), F32),
            pltpu.VMEM((RANK // 2, ROWS), F32),
            pltpu.VMEM((RANK // 2, ROWS), F32),
            pltpu.VMEM((ROWS, COLS), BF16),
            pltpu.VMEM((NX * NY - 1, 8, WIDE), F32),
            pltpu.VMEM((NZ, 8, WIDE), F32),
            pltpu.VMEM((NX * NY, 8, WIDE), F32),
            pltpu.VMEM((RANK, ROWS), F32),
            pltpu.VMEM((RANK, 2 * RANK), F32),
            pltpu.VMEM((RANK // 2, COLS), BF16),
            pltpu.VMEM((NY, 16, HALF), BF16),
            pltpu.VMEM((RANK, COLS), BF16),
            pltpu.VMEM((NZ, 16, HALF), BF16),
            pltpu.SemaphoreType.DMA((5,)),
            pltpu.SemaphoreType.DMA((5,)),
            pltpu.SemaphoreType.DMA((5,)),
            pltpu.SemaphoreType.DMA((8,)),
            pltpu.SemaphoreType.DMA((8,)),
        ],
        compiler_params=pltpu.CompilerParams(
            collective_id=0, has_side_effects=True, vmem_limit_bytes=40 << 20
        ),
        name="sums",
    )(*outside)
    results = [pltpu.with_memory_space_constraint(a, pltpu.VMEM) for a in results]
    return pl.pallas_call(
        update_kernel,
        in_specs=[inside] * 4,
        out_specs=(anywhere, anywhere),
        out_shape=(
            jax.ShapeDtypeStruct((ROWS, COLS), BF16),
            jax.ShapeDtypeStruct((RANK, COLS), F32),
        ),
        scratch_shapes=[
            pltpu.VMEM((ROWS, COLS), BF16),
            pltpu.SemaphoreType.DMA((1 + ROWS // STEP,)),
        ],
        compiler_params=pltpu.CompilerParams(vmem_limit_bytes=40 << 20),
        name="update",
    )(*results)


def solution(mesh):
    return jax.shard_map(
        body,
        mesh=mesh,
        in_specs=(P("dp", None), P("dp", "tensor"), P("dp", "tensor"), P(None, "tensor")),
        out_specs=(P("dp", "tensor"), P(None, "tensor")),
        check_vma=False,
    )
```

```python
import functools

import jax
import jax.numpy as jnp
from jax import lax
from jax.experimental import pallas as pl
from jax.experimental.pallas import tpu as pltpu
from jax.sharding import PartitionSpec as P

ROWS = 1280
COLS = 1280
TOK = 1024
RANK = 64
REPLICAS = 64
NX, NY, NZ = 4, 4, 8
HALF = 640
F32 = jnp.float32
BF16 = jnp.bfloat16
STEP = 256
GROUPS = ROWS // STEP
OWNERS = 2 * GROUPS


def device(x, y, z, c):
    return {"dp": (y * NZ + z) * 2 + c, "tensor": x}


def send(src, dst, send_sem, recv_sem, target):
    pltpu.make_async_remote_copy(
        src_ref=src, dst_ref=dst, send_sem=send_sem, recv_sem=recv_sem,
        device_id=target, device_id_type=pl.DeviceIdType.MESH,
    ).start()


def wait_bytes(ref, sem):
    pltpu.make_async_copy(ref, ref, sem).wait()


def hops(d, n):
    return min(d, n - d)


XY = sorted(
    [(dx, dy) for dx in range(NX) for dy in range(NY) if (dx, dy) != (0, 0)],
    key=lambda d: -(hops(d[0], NX) + hops(d[1], NY)),
)
ZS = sorted(range(1, NZ), key=lambda d: -hops(d, NZ))


def sixteen(i):
    return pl.ds(pl.multiple_of(i * 16, 16), 16)


def lane_half(i):
    return pl.ds(pl.multiple_of(i * HALF, 128), HALF)


def eliminate(first, last, work):
    lane = lax.broadcasted_iota(jnp.int32, (RANK, 2 * RANK), 1)
    row = lax.broadcasted_iota(jnp.int32, (RANK, 2 * RANK), 0)

    def step(k, w):
        pivot_row = jnp.sum(jnp.where(row == k, w, 0.0), axis=0, keepdims=True)
        column = jnp.sum(jnp.where(lane == k, w, 0.0), axis=1, keepdims=True)
        pivot = jnp.sum(
            jnp.where(lane[:1] == k, pivot_row, 0.0), axis=1, keepdims=True
        )
        factor = column / pivot
        return w - jnp.where(row > k, factor * pivot_row, 0.0)

    return lax.fori_loop(first, last, step, work)


def sum_kernel(
    acts, cot, err, q_ref,
    merged, q_new, q_low, basis_out,
    acts_v, cot_v, err_v, q_v, weight, part,
    c0, half, twin, r1, z1, g1, left, proj, work,
    fb, fr, fs, z2,
    in_sem, core_send, core_recv, send_sem, recv_sem,
):
    dp = lax.axis_index("dp")
    x = lax.axis_index("tensor")
    c = lax.rem(dp, 2)
    z = lax.rem(dp // 2, NZ)
    y = dp // (2 * NZ)
    other = 1 - c

    def xy_peer(dx, dy):
        return device(lax.rem(x + dx, NX), lax.rem(y + dy, NY), z, c)

    def z_peer(dz):
        return device(x, y, lax.rem(z + dz, NZ), c)

    sibling = device(x, y, z, other)

    copies = [pltpu.make_async_copy(q_ref, q_v, in_sem.at[0])]

    def plan(pairs):
        for src, dst in pairs:
            copies.append(pltpu.make_async_copy(src, dst, in_sem.at[len(copies)]))

    plan([(cot.at[pl.ds(r, 512)], cot_v.at[pl.ds(r, 512)]) for r in range(0, TOK, 512)])
    plan([(err, err_v)])
    plan([(acts.at[pl.ds(r, 512)], acts_v.at[pl.ds(r, 512)]) for r in range(0, TOK, 512)])
    turn = [0, 0]

    def start_copies(upto):
        while turn[0] < min(upto, len(copies)):
            copies[turn[0]].start()
            turn[0] += 1

    def next_copy():
        copies[turn[1]].wait()
        turn[1] += 1
        start_copies(turn[1] + 3)

    start_copies(4)
    barrier = pltpu.get_barrier_semaphore()

    def greet(target):
        pl.semaphore_signal(barrier, inc=1, device_id=target, device_id_type=pl.DeviceIdType.MESH)

    for dx, dy in XY:
        greet(xy_peer(dx, dy))
    for dz in ZS:
        greet(z_peer(dz))
    greet(sibling)
    for dy in range(1, NY):
        greet(device(x, lax.rem(y + dy, NY), z, other))

    next_copy()
    for r in range(0, TOK, 512):
        next_copy()
        product = lax.dot_general(
            cot_v[r : r + 512, :], q_v[...], (((1,), (1,)), ((), ())), preferred_element_type=F32
        )
        high = product.astype(BF16)
        low = (product - high.astype(F32)).astype(BF16)
        weight[r : r + 512, :] = jnp.concatenate([high, low], axis=1)
    next_copy()
    for r in range(0, ROWS, STEP):
        part[:, r : r + STEP] = lax.dot_general(
            q_v[...], err_v[r : r + STEP, :], (((1,), (1,)), ((), ())),
            preferred_element_type=F32,
        )
    ours = pl.ds(pl.multiple_of(c * 32, 32), 32)
    theirs = pl.ds(pl.multiple_of(other * 32, 32), 32)
    next_copy()
    both = lax.dot_general(
        weight[:512, :], acts_v[:512, :], (((0,), (0,)), ((), ())), preferred_element_type=F32
    )
    part[...] += both[:RANK] + both[RANK:]
    next_copy()
    for i, r in enumerate(range(0, ROWS, STEP)):
        both = lax.dot_general(
            weight[512:, :], acts_v[512:, r : r + STEP], (((0,), (0,)), ((), ())),
            preferred_element_type=F32,
        )
        part[:, r : r + STEP] += both[:RANK] + both[RANK:]
        if i == 0:
            pl.semaphore_wait(barrier, len(XY) + len(ZS) + NY)
        columns = pl.ds(r, STEP)
        send(
            part.at[theirs, columns], c0.at[:, columns], core_send.at[i], core_recv.at[i], sibling
        )
    mine = x * NY + y
    for i in range(GROUPS):
        columns = pl.ds(i * STEP, STEP)
        wait_bytes(c0.at[:, columns], core_recv.at[i])
        half[:, columns] = (part[ours, columns] + c0[:, columns]).astype(BF16)
        for owner in (i, GROUPS + i):

            @pl.when(mine != owner)
            def _():
                send(
                    half.at[pl.ds(owner // GROUPS * 16, 16), columns], r1.at[mine],
                    send_sem.at[0], recv_sem.at[0], device(owner // NY, owner % NY, z, c),
                )

    for r in range(0, ROWS, STEP):
        grad = lax.dot_general(
            acts_v[:, r : r + STEP], cot_v[...], (((0,), (0,)), ((), ())),
            preferred_element_type=F32,
        )
        merged[r : r + STEP, :] = (grad + err_v[r : r + STEP, :].astype(F32)).astype(BF16)
        block = pl.ds(r, STEP)
        send(merged.at[block], twin.at[block], send_sem.at[4], recv_sem.at[4], sibling)

    @pl.when(mine < OWNERS)
    def _():
        r1[mine] = half[
            sixteen(mine // GROUPS), pl.ds(pl.multiple_of(lax.rem(mine, GROUPS) * STEP, STEP), STEP)
        ]
        wait_bytes(r1.at[pl.ds(0, NX * NY - 1)], recv_sem.at[0])
        total = r1[0].astype(F32)
        for i in range(1, NX * NY):
            total = total + r1[i].astype(F32)
        z1[z] = total.astype(BF16)
        for dz in ZS:
            send(z1.at[z], z1.at[z], send_sem.at[1], recv_sem.at[1], z_peer(dz))
        wait_bytes(z1.at[pl.ds(0, NZ - 1)], recv_sem.at[1])
        total = z1[0].astype(F32)
        for i in range(1, NZ):
            total = total + z1[i].astype(F32)
        g1[mine] = total.astype(BF16)
        for dx, dy in XY:
            send(g1.at[mine], g1.at[mine], send_sem.at[2], recv_sem.at[2], xy_peer(dx, dy))
        wait_bytes(g1.at[pl.ds(0, OWNERS - 1)], recv_sem.at[2])

    @pl.when(mine >= OWNERS)
    def _():
        wait_bytes(g1, recv_sem.at[2])

    for owner in range(OWNERS):
        row, column = owner // GROUPS * 16, owner % GROUPS * STEP
        left[row : row + 16, column : column + STEP] = g1[owner]
    send(left, proj.at[ours], send_sem.at[3], recv_sem.at[3], sibling)
    wait_bytes(twin, recv_sem.at[4])
    for h in range(2):
        columns = pl.ds(h * HALF, HALF)
        both = jnp.dot(left[...], merged[:, columns], preferred_element_type=F32)
        both = both + jnp.dot(left[...], twin[:, columns], preferred_element_type=F32)
        fb[:, columns] = both.astype(BF16)
        for dy in (2, 1, 3):
            ty = lax.rem(y + dy, NY)

            @pl.when(lax.rem(ty, 2) == h)
            def _():
                send(
                    fb.at[sixteen(ty // 2), columns], fr.at[y],
                    send_sem.at[5], recv_sem.at[5], device(x, ty, z, c),
                )

    fr[y] = fb[sixteen(y // 2), lane_half(lax.rem(y, 2))]

    proj[ours, :] = left[...]
    wait_bytes(left, recv_sem.at[3])
    gram = lax.dot_general(
        proj[...], proj[...], (((1,), (1,)), ((), ())), preferred_element_type=F32
    )
    eye = (
        lax.broadcasted_iota(jnp.int32, (RANK, RANK), 0)
        == lax.broadcasted_iota(jnp.int32, (RANK, RANK), 1)
    ).astype(F32)
    work[...] = eliminate(0, 12, jnp.concatenate([gram, eye], axis=1))

    wait_bytes(fr.at[pl.ds(0, NY - 1)], recv_sem.at[5])
    total = fr[0].astype(F32)
    for i in range(1, NY):
        total = total + fr[i].astype(F32)
    z2[z] = total.astype(BF16)
    for dz in ZS:
        send(z2.at[z], z2.at[z], send_sem.at[6], recv_sem.at[6], z_peer(dz))
    work[...] = eliminate(12, 46, work[...])
    wait_bytes(z2.at[pl.ds(0, NZ - 1)], recv_sem.at[6])
    total = z2[0].astype(F32)
    for i in range(1, NZ):
        total = total + z2[i].astype(F32)
    here = fs.at[sixteen(2 * c + y // 2), lane_half(lax.rem(y, 2))]
    landed = z2.at[pl.ds(0, NZ - 1)]
    here[...] = total.astype(BF16)
    for dy in (2, 1, 3):
        ty = lax.rem(y + dy, NY)
        for core in (other, c):
            send(
                here, here,
                send_sem.at[7], recv_sem.at[7], device(x, ty, z, core),
            )
    send(here, here, send_sem.at[7], recv_sem.at[7], sibling)

    eliminated = eliminate(46, RANK, work[...])
    diagonal = jnp.sum(eliminated[:, :RANK] * eye, axis=1, keepdims=True)
    inverse = eliminated[:, RANK:] * lax.rsqrt(diagonal)
    high = inverse.astype(BF16)
    low = (inverse - high.astype(F32)).astype(BF16)
    split = jnp.concatenate([high, low], axis=0)
    both = jnp.dot(split, proj[...], preferred_element_type=F32)
    basis_out[...] = (both[:RANK] + both[RANK:]).astype(BF16)

    wait_bytes(landed, recv_sem.at[7])
    both = jnp.dot(split, fs[...], preferred_element_type=F32)
    q = (both[:RANK] + both[RANK:]) * (1.0 / REPLICAS)
    q_new[...] = q
    q_low[...] = q.astype(BF16)


    for i, r in enumerate(range(0, ROWS, STEP)):
        wait_bytes(c0.at[:, pl.ds(r, STEP)], core_send.at[i])
    @pl.when(mine < OWNERS)
    def _():
        wait_bytes(r1.at[pl.ds(0, OWNERS - 1)], send_sem.at[0])
        wait_bytes(z1.at[pl.ds(0, NZ - 1)], send_sem.at[1])
        wait_bytes(r1.at[pl.ds(0, NX * NY - 1)], send_sem.at[2])

    @pl.when(mine >= OWNERS)
    def _():
        wait_bytes(r1.at[pl.ds(0, OWNERS)], send_sem.at[0])

    wait_bytes(left, send_sem.at[3])
    wait_bytes(twin, send_sem.at[4])
    wait_bytes(fr.at[pl.ds(0, NY - 1)], send_sem.at[5])
    wait_bytes(z2.at[pl.ds(0, NZ - 1)], send_sem.at[6])
    wait_bytes(landed, send_sem.at[7])


def update_kernel(merged, q_in, q_low, basis, error_new, q_new, error_v, sem):
    copies = [pltpu.make_async_copy(q_in, q_new, sem.at[0])]
    copies[0].start()
    for r in range(0, ROWS, STEP):
        low_rank = lax.dot_general(
            basis[:, r : r + STEP], q_low[...], (((0,), (0,)), ((), ())),
            preferred_element_type=F32,
        )
        error_v[r : r + STEP, :] = (merged[r : r + STEP, :].astype(F32) - low_rank).astype(BF16)
        block = pl.ds(r, STEP)
        copies.append(
            pltpu.make_async_copy(error_v.at[block], error_new.at[block], sem.at[len(copies)])
        )
        copies[-1].start()
    for copy in copies:
        copy.wait()


def body(acts, cotangent, error_prev, q_prev):
    anywhere = pl.BlockSpec(memory_space=pl.ANY)
    inside = pl.BlockSpec(memory_space=pltpu.VMEM)
    outside = [
        pltpu.with_memory_space_constraint(a, pltpu.HBM)
        for a in (acts, cotangent, error_prev, q_prev)
    ]
    results = pl.pallas_call(
        sum_kernel,
        out_shape=(
            pltpu.VMEM((ROWS, COLS), BF16),
            pltpu.VMEM((RANK, COLS), F32),
            pltpu.VMEM((RANK, COLS), BF16),
            pltpu.VMEM((RANK, ROWS), BF16),
        ),
        in_specs=[anywhere] * 4,
        out_specs=(inside,) * 4,
        scratch_shapes=[
            pltpu.VMEM((TOK, ROWS), BF16),
            pltpu.VMEM((TOK, COLS), BF16),
            pltpu.VMEM((ROWS, COLS), BF16),
            pltpu.VMEM((RANK, COLS), BF16),
            pltpu.VMEM((TOK, 2 * RANK), BF16),
            pltpu.VMEM((RANK, ROWS), F32),
            pltpu.VMEM((RANK // 2, ROWS), F32),
            pltpu.VMEM((RANK // 2, ROWS), BF16),
            pltpu.VMEM((ROWS, COLS), BF16),
            pltpu.VMEM((NX * NY, 16, STEP), BF16),
            pltpu.VMEM((NZ, 16, STEP), BF16),
            pltpu.VMEM((OWNERS, 16, STEP), BF16),
            pltpu.VMEM((RANK // 2, ROWS), BF16),
            pltpu.VMEM((RANK, ROWS), BF16),
            pltpu.VMEM((RANK, 2 * RANK), F32),
            pltpu.VMEM((RANK // 2, COLS), BF16),
            pltpu.VMEM((NY, 16, HALF), BF16),
            pltpu.VMEM((RANK, COLS), BF16),
            pltpu.VMEM((NZ, 16, HALF), BF16),
            pltpu.SemaphoreType.DMA((6,)),
            pltpu.SemaphoreType.DMA((GROUPS,)),
            pltpu.SemaphoreType.DMA((GROUPS,)),
            pltpu.SemaphoreType.DMA((8,)),
            pltpu.SemaphoreType.DMA((8,)),
        ],
        compiler_params=pltpu.CompilerParams(
            collective_id=0, has_side_effects=True, vmem_limit_bytes=40 << 20
        ),
        name="sums",
    )(*outside)
    results = [pltpu.with_memory_space_constraint(a, pltpu.VMEM) for a in results]
    return pl.pallas_call(
        update_kernel,
        in_specs=[inside] * 4,
        out_specs=(anywhere, anywhere),
        out_shape=(
            jax.ShapeDtypeStruct((ROWS, COLS), BF16),
            jax.ShapeDtypeStruct((RANK, COLS), F32),
        ),
        scratch_shapes=[
            pltpu.VMEM((ROWS, COLS), BF16),
            pltpu.SemaphoreType.DMA((1 + ROWS // STEP,)),
        ],
        compiler_params=pltpu.CompilerParams(vmem_limit_bytes=40 << 20),
        name="update",
    )(*results)


def solution(mesh):
    return jax.shard_map(
        body,
        mesh=mesh,
        in_specs=(P("dp", None), P("dp", "tensor"), P("dp", "tensor"), P(None, "tensor")),
        out_specs=(P("dp", "tensor"), P(None, "tensor")),
        check_vma=False,
    )
```

```python
import functools

import jax
import jax.numpy as jnp
from jax import lax
from jax.experimental import pallas as pl
from jax.experimental.pallas import tpu as pltpu
from jax.sharding import PartitionSpec as P

ROWS = 1280
COLS = 1280
TOK = 1024
RANK = 64
REPLICAS = 64
NX, NY, NZ = 4, 4, 8
HALF = 640
F32 = jnp.float32
BF16 = jnp.bfloat16
STEP = 256
GROUPS = ROWS // STEP
OWNERS = 2 * GROUPS


def device(x, y, z, c):
    return {"dp": (y * NZ + z) * 2 + c, "tensor": x}


def send(src, dst, send_sem, recv_sem, target):
    pltpu.make_async_remote_copy(
        src_ref=src, dst_ref=dst, send_sem=send_sem, recv_sem=recv_sem,
        device_id=target, device_id_type=pl.DeviceIdType.MESH,
    ).start()


def wait_bytes(ref, sem):
    pltpu.make_async_copy(ref, ref, sem).wait()


def hops(d, n):
    return min(d, n - d)


XY = sorted(
    [(dx, dy) for dx in range(NX) for dy in range(NY) if (dx, dy) != (0, 0)],
    key=lambda d: -(hops(d[0], NX) + hops(d[1], NY)),
)
ZS = sorted(range(1, NZ), key=lambda d: -hops(d, NZ))


def place(owner):
    return owner * 8 // 5


def sixteen(i):
    return pl.ds(pl.multiple_of(i * 16, 16), 16)


def lane_half(i):
    return pl.ds(pl.multiple_of(i * HALF, 128), HALF)


def eliminate(first, last, work):
    lane = lax.broadcasted_iota(jnp.int32, (RANK, 2 * RANK), 1)
    row = lax.broadcasted_iota(jnp.int32, (RANK, 2 * RANK), 0)

    def step(k, w):
        pivot_row = jnp.sum(jnp.where(row == k, w, 0.0), axis=0, keepdims=True)
        column = jnp.sum(jnp.where(lane == k, w, 0.0), axis=1, keepdims=True)
        pivot = jnp.sum(
            jnp.where(lane[:1] == k, pivot_row, 0.0), axis=1, keepdims=True
        )
        factor = column / pivot
        return w - jnp.where(row > k, factor * pivot_row, 0.0)

    return lax.fori_loop(first, last, step, work)


def sum_kernel(
    acts, cot, err, q_ref,
    merged, q_new, q_low, basis_out,
    acts_v, cot_v, err_v, q_v, weight, part,
    c0, half, twin, r1, z1, g1, left, proj, work,
    fb, fr, fs, z2,
    in_sem, core_send, core_recv, send_sem, recv_sem,
):
    dp = lax.axis_index("dp")
    x = lax.axis_index("tensor")
    c = lax.rem(dp, 2)
    z = lax.rem(dp // 2, NZ)
    y = dp // (2 * NZ)
    other = 1 - c

    def xy_peer(dx, dy):
        return device(lax.rem(x + dx, NX), lax.rem(y + dy, NY), z, c)

    def z_peer(dz):
        return device(x, y, lax.rem(z + dz, NZ), c)

    sibling = device(x, y, z, other)

    copies = [pltpu.make_async_copy(q_ref, q_v, in_sem.at[0])]

    def plan(pairs):
        for src, dst in pairs:
            copies.append(pltpu.make_async_copy(src, dst, in_sem.at[len(copies)]))

    plan([(cot.at[pl.ds(r, 512)], cot_v.at[pl.ds(r, 512)]) for r in range(0, TOK, 512)])
    plan([(err, err_v)])
    plan([(acts.at[pl.ds(r, 512)], acts_v.at[pl.ds(r, 512)]) for r in range(0, TOK, 512)])
    turn = [0, 0]

    def start_copies(upto):
        while turn[0] < min(upto, len(copies)):
            copies[turn[0]].start()
            turn[0] += 1

    def next_copy():
        copies[turn[1]].wait()
        turn[1] += 1
        start_copies(turn[1] + 3)

    start_copies(4)
    barrier = pltpu.get_barrier_semaphore()

    def greet(target):
        pl.semaphore_signal(barrier, inc=1, device_id=target, device_id_type=pl.DeviceIdType.MESH)

    for dx, dy in XY:
        greet(xy_peer(dx, dy))
    for dz in ZS:
        greet(z_peer(dz))
    greet(sibling)
    for dy in range(1, NY):
        greet(device(x, lax.rem(y + dy, NY), z, other))

    next_copy()
    for r in range(0, TOK, 512):
        next_copy()
        product = lax.dot_general(
            cot_v[r : r + 512, :], q_v[...], (((1,), (1,)), ((), ())), preferred_element_type=F32
        )
        high = product.astype(BF16)
        low = (product - high.astype(F32)).astype(BF16)
        weight[r : r + 512, :] = jnp.concatenate([high, low], axis=1)
    next_copy()
    for r in range(0, ROWS, STEP):
        part[:, r : r + STEP] = lax.dot_general(
            q_v[...], err_v[r : r + STEP, :], (((1,), (1,)), ((), ())),
            preferred_element_type=F32,
        )
    ours = pl.ds(pl.multiple_of(c * 32, 32), 32)
    theirs = pl.ds(pl.multiple_of(other * 32, 32), 32)
    next_copy()
    both = lax.dot_general(
        weight[:512, :], acts_v[:512, :], (((0,), (0,)), ((), ())), preferred_element_type=F32
    )
    part[...] += both[:RANK] + both[RANK:]
    next_copy()
    for i, r in enumerate(range(0, ROWS, STEP)):
        both = lax.dot_general(
            weight[512:, :], acts_v[512:, r : r + STEP], (((0,), (0,)), ((), ())),
            preferred_element_type=F32,
        )
        part[:, r : r + STEP] += both[:RANK] + both[RANK:]
        if i == 0:
            pl.semaphore_wait(barrier, len(XY) + len(ZS) + NY)
        columns = pl.ds(r, STEP)
        send(
            part.at[theirs, columns], c0.at[:, columns], core_send.at[i], core_recv.at[i], sibling
        )
    mine = x * NY + y
    held = (mine * 5 + 7) // 8
    owns = place(held) == mine
    foreign = place(held) != mine
    for i in range(GROUPS):
        columns = pl.ds(i * STEP, STEP)
        wait_bytes(c0.at[:, columns], core_recv.at[i])
        half[:, columns] = (part[ours, columns] + c0[:, columns]).astype(BF16)
        for owner in (i, GROUPS + i):

            @pl.when(mine != place(owner))
            def _():
                send(
                    half.at[pl.ds(owner // GROUPS * 16, 16), columns], r1.at[mine],
                    send_sem.at[0], recv_sem.at[0], device(place(owner) // NY, place(owner) % NY, z, c),
                )

    def merge(first, last):
        for r in range(first, last, STEP):
            grad = lax.dot_general(
                acts_v[:, r : r + STEP], cot_v[...], (((0,), (0,)), ((), ())),
                preferred_element_type=F32,
            )
            merged[r : r + STEP, :] = (grad + err_v[r : r + STEP, :].astype(F32)).astype(BF16)
            rows = pl.ds(r, STEP)
            send(merged.at[rows], twin.at[rows], send_sem.at[4], recv_sem.at[4], sibling)

    merge(0, 2 * STEP)

    @pl.when(owns)
    def _():
        r1[mine] = half[
            sixteen(held // GROUPS), pl.ds(pl.multiple_of(lax.rem(held, GROUPS) * STEP, STEP), STEP)
        ]
        wait_bytes(r1.at[pl.ds(0, NX * NY - 1)], recv_sem.at[0])
        total = r1[0].astype(F32)
        for i in range(1, NX * NY):
            total = total + r1[i].astype(F32)
        z1[z] = total.astype(BF16)
        for dz in ZS:
            send(z1.at[z], z1.at[z], send_sem.at[1], recv_sem.at[1], z_peer(dz))

    merge(2 * STEP, ROWS)

    @pl.when(owns)
    def _():
        wait_bytes(z1.at[pl.ds(0, NZ - 1)], recv_sem.at[1])
        total = z1[0].astype(F32)
        for i in range(1, NZ):
            total = total + z1[i].astype(F32)
        g1[held] = total.astype(BF16)
        for dx, dy in XY:
            send(g1.at[held], g1.at[held], send_sem.at[2], recv_sem.at[2], xy_peer(dx, dy))
        wait_bytes(g1.at[pl.ds(0, OWNERS - 1)], recv_sem.at[2])

    @pl.when(foreign)
    def _():
        wait_bytes(g1, recv_sem.at[2])

    for owner in range(OWNERS):
        row, column = owner // GROUPS * 16, owner % GROUPS * STEP
        left[row : row + 16, column : column + STEP] = g1[owner]
    send(left, proj.at[ours], send_sem.at[3], recv_sem.at[3], sibling)
    wait_bytes(twin, recv_sem.at[4])
    for h in range(2):
        columns = pl.ds(h * HALF, HALF)
        both = jnp.dot(left[...], merged[:, columns], preferred_element_type=F32)
        both = both + jnp.dot(left[...], twin[:, columns], preferred_element_type=F32)
        fb[:, columns] = both.astype(BF16)
        for dy in (2, 1, 3):
            ty = lax.rem(y + dy, NY)

            @pl.when(lax.rem(ty, 2) == h)
            def _():
                send(
                    fb.at[sixteen(ty // 2), columns], fr.at[y],
                    send_sem.at[5], recv_sem.at[5], device(x, ty, z, c),
                )

    fr[y] = fb[sixteen(y // 2), lane_half(lax.rem(y, 2))]

    proj[ours, :] = left[...]
    wait_bytes(left, recv_sem.at[3])
    gram = lax.dot_general(
        proj[...], proj[...], (((1,), (1,)), ((), ())), preferred_element_type=F32
    )
    eye = (
        lax.broadcasted_iota(jnp.int32, (RANK, RANK), 0)
        == lax.broadcasted_iota(jnp.int32, (RANK, RANK), 1)
    ).astype(F32)
    work[...] = eliminate(0, 12, jnp.concatenate([gram, eye], axis=1))

    wait_bytes(fr.at[pl.ds(0, NY - 1)], recv_sem.at[5])
    total = fr[0].astype(F32)
    for i in range(1, NY):
        total = total + fr[i].astype(F32)
    z2[z] = total.astype(BF16)
    for dz in ZS:
        send(z2.at[z], z2.at[z], send_sem.at[6], recv_sem.at[6], z_peer(dz))
    work[...] = eliminate(12, 46, work[...])
    wait_bytes(z2.at[pl.ds(0, NZ - 1)], recv_sem.at[6])
    total = z2[0].astype(F32)
    for i in range(1, NZ):
        total = total + z2[i].astype(F32)
    here = fs.at[sixteen(2 * c + y // 2), lane_half(lax.rem(y, 2))]
    landed = z2.at[pl.ds(0, NZ - 1)]
    here[...] = total.astype(BF16)
    for dy in (2, 1, 3):
        ty = lax.rem(y + dy, NY)
        for core in (other, c):
            send(
                here, here,
                send_sem.at[7], recv_sem.at[7], device(x, ty, z, core),
            )
    send(here, here, send_sem.at[7], recv_sem.at[7], sibling)

    eliminated = eliminate(46, RANK, work[...])
    diagonal = jnp.sum(eliminated[:, :RANK] * eye, axis=1, keepdims=True)
    inverse = eliminated[:, RANK:] * lax.rsqrt(diagonal)
    high = inverse.astype(BF16)
    low = (inverse - high.astype(F32)).astype(BF16)
    split = jnp.concatenate([high, low], axis=0)
    both = jnp.dot(split, proj[...], preferred_element_type=F32)
    basis_out[...] = (both[:RANK] + both[RANK:]).astype(BF16)

    wait_bytes(landed, recv_sem.at[7])
    both = jnp.dot(split, fs[...], preferred_element_type=F32)
    q = (both[:RANK] + both[RANK:]) * (1.0 / REPLICAS)
    q_new[...] = q
    q_low[...] = q.astype(BF16)


    for i, r in enumerate(range(0, ROWS, STEP)):
        wait_bytes(c0.at[:, pl.ds(r, STEP)], core_send.at[i])
    @pl.when(owns)
    def _():
        wait_bytes(r1.at[pl.ds(0, OWNERS - 1)], send_sem.at[0])
        wait_bytes(z1.at[pl.ds(0, NZ - 1)], send_sem.at[1])
        wait_bytes(r1.at[pl.ds(0, NX * NY - 1)], send_sem.at[2])

    @pl.when(foreign)
    def _():
        wait_bytes(r1.at[pl.ds(0, OWNERS)], send_sem.at[0])

    wait_bytes(left, send_sem.at[3])
    wait_bytes(twin, send_sem.at[4])
    wait_bytes(fr.at[pl.ds(0, NY - 1)], send_sem.at[5])
    wait_bytes(z2.at[pl.ds(0, NZ - 1)], send_sem.at[6])
    wait_bytes(landed, send_sem.at[7])


def update_kernel(merged, q_in, q_low, basis, error_new, q_new, error_v, sem):
    copies = [pltpu.make_async_copy(q_in, q_new, sem.at[0])]
    copies[0].start()
    for r in range(0, ROWS, STEP):
        low_rank = lax.dot_general(
            basis[:, r : r + STEP], q_low[...], (((0,), (0,)), ((), ())),
            preferred_element_type=F32,
        )
        error_v[r : r + STEP, :] = (merged[r : r + STEP, :].astype(F32) - low_rank).astype(BF16)
        block = pl.ds(r, STEP)
        copies.append(
            pltpu.make_async_copy(error_v.at[block], error_new.at[block], sem.at[len(copies)])
        )
        copies[-1].start()
    for copy in copies:
        copy.wait()


def body(acts, cotangent, error_prev, q_prev):
    anywhere = pl.BlockSpec(memory_space=pl.ANY)
    inside = pl.BlockSpec(memory_space=pltpu.VMEM)
    outside = [
        pltpu.with_memory_space_constraint(a, pltpu.HBM)
        for a in (acts, cotangent, error_prev, q_prev)
    ]
    results = pl.pallas_call(
        sum_kernel,
        out_shape=(
            pltpu.VMEM((ROWS, COLS), BF16),
            pltpu.VMEM((RANK, COLS), F32),
            pltpu.VMEM((RANK, COLS), BF16),
            pltpu.VMEM((RANK, ROWS), BF16),
        ),
        in_specs=[anywhere] * 4,
        out_specs=(inside,) * 4,
        scratch_shapes=[
            pltpu.VMEM((TOK, ROWS), BF16),
            pltpu.VMEM((TOK, COLS), BF16),
            pltpu.VMEM((ROWS, COLS), BF16),
            pltpu.VMEM((RANK, COLS), BF16),
            pltpu.VMEM((TOK, 2 * RANK), BF16),
            pltpu.VMEM((RANK, ROWS), F32),
            pltpu.VMEM((RANK // 2, ROWS), F32),
            pltpu.VMEM((RANK // 2, ROWS), BF16),
            pltpu.VMEM((ROWS, COLS), BF16),
            pltpu.VMEM((NX * NY, 16, STEP), BF16),
            pltpu.VMEM((NZ, 16, STEP), BF16),
            pltpu.VMEM((OWNERS, 16, STEP), BF16),
            pltpu.VMEM((RANK // 2, ROWS), BF16),
            pltpu.VMEM((RANK, ROWS), BF16),
            pltpu.VMEM((RANK, 2 * RANK), F32),
            pltpu.VMEM((RANK // 2, COLS), BF16),
            pltpu.VMEM((NY, 16, HALF), BF16),
            pltpu.VMEM((RANK, COLS), BF16),
            pltpu.VMEM((NZ, 16, HALF), BF16),
            pltpu.SemaphoreType.DMA((6,)),
            pltpu.SemaphoreType.DMA((GROUPS,)),
            pltpu.SemaphoreType.DMA((GROUPS,)),
            pltpu.SemaphoreType.DMA((8,)),
            pltpu.SemaphoreType.DMA((8,)),
        ],
        compiler_params=pltpu.CompilerParams(
            collective_id=0, has_side_effects=True, vmem_limit_bytes=40 << 20
        ),
        name="sums",
    )(*outside)
    results = [pltpu.with_memory_space_constraint(a, pltpu.VMEM) for a in results]
    return pl.pallas_call(
        update_kernel,
        in_specs=[inside] * 4,
        out_specs=(anywhere, anywhere),
        out_shape=(
            jax.ShapeDtypeStruct((ROWS, COLS), BF16),
            jax.ShapeDtypeStruct((RANK, COLS), F32),
        ),
        scratch_shapes=[
            pltpu.VMEM((ROWS, COLS), BF16),
            pltpu.SemaphoreType.DMA((1 + ROWS // STEP,)),
        ],
        compiler_params=pltpu.CompilerParams(vmem_limit_bytes=40 << 20),
        name="update",
    )(*results)


def solution(mesh):
    return jax.shard_map(
        body,
        mesh=mesh,
        in_specs=(P("dp", None), P("dp", "tensor"), P("dp", "tensor"), P(None, "tensor")),
        out_specs=(P("dp", "tensor"), P(None, "tensor")),
        check_vma=False,
    )
```

```python
import functools

import jax
import jax.numpy as jnp
from jax import lax
from jax.experimental import pallas as pl
from jax.experimental.pallas import tpu as pltpu
from jax.sharding import PartitionSpec as P

ROWS = 1280
COLS = 1280
TOK = 1024
RANK = 64
REPLICAS = 64
NX, NY, NZ = 4, 4, 8
HALF = 640
F32 = jnp.float32
BF16 = jnp.bfloat16
STEP = 256
GROUPS = ROWS // STEP
OWNERS = 2 * GROUPS


def device(x, y, z, c):
    return {"dp": (y * NZ + z) * 2 + c, "tensor": x}


def send(src, dst, send_sem, recv_sem, target):
    pltpu.make_async_remote_copy(
        src_ref=src, dst_ref=dst, send_sem=send_sem, recv_sem=recv_sem,
        device_id=target, device_id_type=pl.DeviceIdType.MESH,
    ).start()


def wait_bytes(ref, sem):
    pltpu.make_async_copy(ref, ref, sem).wait()


def hops(d, n):
    return min(d, n - d)


XY = sorted(
    [(dx, dy) for dx in range(NX) for dy in range(NY) if (dx, dy) != (0, 0)],
    key=lambda d: -(hops(d[0], NX) + hops(d[1], NY)),
)
ZS = sorted(range(1, NZ), key=lambda d: -hops(d, NZ))


def place(owner):
    return owner * 8 // 5


def sixteen(i):
    return pl.ds(pl.multiple_of(i * 16, 16), 16)


def lane_half(i):
    return pl.ds(pl.multiple_of(i * HALF, 128), HALF)


def eliminate(first, last, work):
    lane = lax.broadcasted_iota(jnp.int32, (RANK, 2 * RANK), 1)
    row = lax.broadcasted_iota(jnp.int32, (RANK, 2 * RANK), 0)

    def step(k, w):
        pivot_row = jnp.sum(jnp.where(row == k, w, 0.0), axis=0, keepdims=True)
        column = jnp.sum(jnp.where(lane == k, w, 0.0), axis=1, keepdims=True)
        pivot = jnp.sum(
            jnp.where(lane[:1] == k, pivot_row, 0.0), axis=1, keepdims=True
        )
        factor = column / pivot
        return w - jnp.where(row > k, factor * pivot_row, 0.0)

    return lax.fori_loop(first, last, step, work)


def sum_kernel(
    acts, cot, err, q_ref,
    merged, q_new, q_low, basis_out,
    acts_v, cot_v, err_v, q_v, weight, part,
    half, twin, r1, z1, g1, left, proj, work,
    fb, fr, fs, z2,
    in_sem, send_sem, recv_sem,
):
    dp = lax.axis_index("dp")
    x = lax.axis_index("tensor")
    c = lax.rem(dp, 2)
    z = lax.rem(dp // 2, NZ)
    y = dp // (2 * NZ)
    other = 1 - c

    def xy_peer(dx, dy):
        return device(lax.rem(x + dx, NX), lax.rem(y + dy, NY), z, c)

    def z_peer(dz):
        return device(x, y, lax.rem(z + dz, NZ), c)

    sibling = device(x, y, z, other)

    copies = [pltpu.make_async_copy(q_ref, q_v, in_sem.at[0])]

    def plan(pairs):
        for src, dst in pairs:
            copies.append(pltpu.make_async_copy(src, dst, in_sem.at[len(copies)]))

    plan([(cot.at[pl.ds(r, 512)], cot_v.at[pl.ds(r, 512)]) for r in range(0, TOK, 512)])
    plan([(err, err_v)])
    plan([(acts.at[pl.ds(r, 512)], acts_v.at[pl.ds(r, 512)]) for r in range(0, TOK, 512)])
    turn = [0, 0]

    def start_copies(upto):
        while turn[0] < min(upto, len(copies)):
            copies[turn[0]].start()
            turn[0] += 1

    def next_copy():
        copies[turn[1]].wait()
        turn[1] += 1
        start_copies(turn[1] + 3)

    start_copies(4)
    barrier = pltpu.get_barrier_semaphore()

    def greet(target):
        pl.semaphore_signal(barrier, inc=1, device_id=target, device_id_type=pl.DeviceIdType.MESH)

    for dx, dy in XY:
        greet(xy_peer(dx, dy))
    for dz in ZS:
        greet(z_peer(dz))
    greet(sibling)
    for dx, dy in XY:
        greet(device(lax.rem(x + dx, NX), lax.rem(y + dy, NY), z, other))

    next_copy()
    for r in range(0, TOK, 512):
        next_copy()
        product = lax.dot_general(
            cot_v[r : r + 512, :], q_v[...], (((1,), (1,)), ((), ())), preferred_element_type=F32
        )
        high = product.astype(BF16)
        low = (product - high.astype(F32)).astype(BF16)
        weight[r : r + 512, :] = jnp.concatenate([high, low], axis=1)
    next_copy()
    for r in range(0, ROWS, STEP):
        part[:, r : r + STEP] = lax.dot_general(
            q_v[...], err_v[r : r + STEP, :], (((1,), (1,)), ((), ())),
            preferred_element_type=F32,
        )
    ours = pl.ds(pl.multiple_of(c * 32, 32), 32)
    mine = x * NY + y
    held = (mine * 5 + 7) // 8
    owns = place(held) == mine
    foreign = place(held) != mine
    next_copy()
    both = lax.dot_general(
        weight[:512, :], acts_v[:512, :], (((0,), (0,)), ((), ())), preferred_element_type=F32
    )
    part[...] += both[:RANK] + both[RANK:]
    next_copy()
    for i, r in enumerate(range(0, ROWS, STEP)):
        both = lax.dot_general(
            weight[512:, :], acts_v[512:, r : r + STEP], (((0,), (0,)), ((), ())),
            preferred_element_type=F32,
        )
        part[:, r : r + STEP] += both[:RANK] + both[RANK:]
        if i == 0:
            pl.semaphore_wait(barrier, 2 * len(XY) + len(ZS) + 1)
        columns = pl.ds(r, STEP)
        half[:, columns] = part[:, columns].astype(BF16)
        for core in range(2):
            for owner in (i, GROUPS + i):

                @pl.when(jnp.logical_or(mine != place(owner), c != core))
                def _():
                    send(
                        half.at[pl.ds(core * 32 + owner // GROUPS * 16, 16), columns],
                        r1.at[mine * 2 + c], send_sem.at[0], recv_sem.at[0],
                        device(place(owner) // NY, place(owner) % NY, z, core),
                    )

    def merge(first, last):
        for r in range(first, last, STEP):
            grad = lax.dot_general(
                acts_v[:, r : r + STEP], cot_v[...], (((0,), (0,)), ((), ())),
                preferred_element_type=F32,
            )
            merged[r : r + STEP, :] = (grad + err_v[r : r + STEP, :].astype(F32)).astype(BF16)
            rows = pl.ds(r, STEP)
            send(merged.at[rows], twin.at[rows], send_sem.at[4], recv_sem.at[4], sibling)

    merge(0, 2 * STEP)

    @pl.when(owns)
    def _():
        r1[mine * 2 + c] = half[
            sixteen(2 * c + held // GROUPS), pl.ds(pl.multiple_of(lax.rem(held, GROUPS) * STEP, STEP), STEP)
        ]
        wait_bytes(r1.at[pl.ds(0, 2 * NX * NY - 1)], recv_sem.at[0])
        total = r1[0].astype(F32)
        for i in range(1, 2 * NX * NY):
            total = total + r1[i].astype(F32)
        z1[z] = total.astype(BF16)
        for dz in ZS:
            send(z1.at[z], z1.at[z], send_sem.at[1], recv_sem.at[1], z_peer(dz))

    merge(2 * STEP, ROWS)

    @pl.when(owns)
    def _():
        wait_bytes(z1.at[pl.ds(0, NZ - 1)], recv_sem.at[1])
        total = z1[0].astype(F32)
        for i in range(1, NZ):
            total = total + z1[i].astype(F32)
        g1[held] = total.astype(BF16)
        for dx, dy in XY:
            send(g1.at[held], g1.at[held], send_sem.at[2], recv_sem.at[2], xy_peer(dx, dy))
        wait_bytes(g1.at[pl.ds(0, OWNERS - 1)], recv_sem.at[2])

    @pl.when(foreign)
    def _():
        wait_bytes(g1, recv_sem.at[2])

    for owner in range(OWNERS):
        row, column = owner // GROUPS * 16, owner % GROUPS * STEP
        left[row : row + 16, column : column + STEP] = g1[owner]
    send(left, proj.at[ours], send_sem.at[3], recv_sem.at[3], sibling)
    wait_bytes(twin, recv_sem.at[4])
    for h in range(2):
        columns = pl.ds(h * HALF, HALF)
        both = jnp.dot(left[...], merged[:, columns], preferred_element_type=F32)
        both = both + jnp.dot(left[...], twin[:, columns], preferred_element_type=F32)
        fb[:, columns] = both.astype(BF16)
        for dy in (2, 1, 3):
            ty = lax.rem(y + dy, NY)

            @pl.when(lax.rem(ty, 2) == h)
            def _():
                send(
                    fb.at[sixteen(ty // 2), columns], fr.at[y],
                    send_sem.at[5], recv_sem.at[5], device(x, ty, z, c),
                )

    fr[y] = fb[sixteen(y // 2), lane_half(lax.rem(y, 2))]

    proj[ours, :] = left[...]
    wait_bytes(left, recv_sem.at[3])
    gram = lax.dot_general(
        proj[...], proj[...], (((1,), (1,)), ((), ())), preferred_element_type=F32
    )
    eye = (
        lax.broadcasted_iota(jnp.int32, (RANK, RANK), 0)
        == lax.broadcasted_iota(jnp.int32, (RANK, RANK), 1)
    ).astype(F32)
    work[...] = eliminate(0, 12, jnp.concatenate([gram, eye], axis=1))

    wait_bytes(fr.at[pl.ds(0, NY - 1)], recv_sem.at[5])
    total = fr[0].astype(F32)
    for i in range(1, NY):
        total = total + fr[i].astype(F32)
    z2[z] = total.astype(BF16)
    for dz in ZS:
        send(z2.at[z], z2.at[z], send_sem.at[6], recv_sem.at[6], z_peer(dz))
    work[...] = eliminate(12, 46, work[...])
    wait_bytes(z2.at[pl.ds(0, NZ - 1)], recv_sem.at[6])
    total = z2[0].astype(F32)
    for i in range(1, NZ):
        total = total + z2[i].astype(F32)
    here = fs.at[sixteen(2 * c + y // 2), lane_half(lax.rem(y, 2))]
    landed = z2.at[pl.ds(0, NZ - 1)]
    here[...] = total.astype(BF16)
    for dy in (2, 1, 3):
        ty = lax.rem(y + dy, NY)
        for core in (other, c):
            send(
                here, here,
                send_sem.at[7], recv_sem.at[7], device(x, ty, z, core),
            )
    send(here, here, send_sem.at[7], recv_sem.at[7], sibling)

    eliminated = eliminate(46, RANK, work[...])
    diagonal = jnp.sum(eliminated[:, :RANK] * eye, axis=1, keepdims=True)
    inverse = eliminated[:, RANK:] * lax.rsqrt(diagonal)
    high = inverse.astype(BF16)
    low = (inverse - high.astype(F32)).astype(BF16)
    split = jnp.concatenate([high, low], axis=0)
    both = jnp.dot(split, proj[...], preferred_element_type=F32)
    basis_out[...] = (both[:RANK] + both[RANK:]).astype(BF16)

    wait_bytes(landed, recv_sem.at[7])
    both = jnp.dot(split, fs[...], preferred_element_type=F32)
    q = (both[:RANK] + both[RANK:]) * (1.0 / REPLICAS)
    q_new[...] = q
    q_low[...] = q.astype(BF16)


    @pl.when(owns)
    def _():
        wait_bytes(r1.at[pl.ds(0, 2 * OWNERS - 1)], send_sem.at[0])
        wait_bytes(z1.at[pl.ds(0, NZ - 1)], send_sem.at[1])
        wait_bytes(r1.at[pl.ds(0, NX * NY - 1)], send_sem.at[2])

    @pl.when(foreign)
    def _():
        wait_bytes(r1.at[pl.ds(0, 2 * OWNERS)], send_sem.at[0])

    wait_bytes(left, send_sem.at[3])
    wait_bytes(twin, send_sem.at[4])
    wait_bytes(fr.at[pl.ds(0, NY - 1)], send_sem.at[5])
    wait_bytes(z2.at[pl.ds(0, NZ - 1)], send_sem.at[6])
    wait_bytes(landed, send_sem.at[7])


def update_kernel(merged, q_in, q_low, basis, error_new, q_new, error_v, sem):
    copies = [pltpu.make_async_copy(q_in, q_new, sem.at[0])]
    copies[0].start()
    for r in range(0, ROWS, STEP):
        low_rank = lax.dot_general(
            basis[:, r : r + STEP], q_low[...], (((0,), (0,)), ((), ())),
            preferred_element_type=F32,
        )
        error_v[r : r + STEP, :] = (merged[r : r + STEP, :].astype(F32) - low_rank).astype(BF16)
        block = pl.ds(r, STEP)
        copies.append(
            pltpu.make_async_copy(error_v.at[block], error_new.at[block], sem.at[len(copies)])
        )
        copies[-1].start()
    for copy in copies:
        copy.wait()


def body(acts, cotangent, error_prev, q_prev):
    anywhere = pl.BlockSpec(memory_space=pl.ANY)
    inside = pl.BlockSpec(memory_space=pltpu.VMEM)
    outside = [
        pltpu.with_memory_space_constraint(a, pltpu.HBM)
        for a in (acts, cotangent, error_prev, q_prev)
    ]
    results = pl.pallas_call(
        sum_kernel,
        out_shape=(
            pltpu.VMEM((ROWS, COLS), BF16),
            pltpu.VMEM((RANK, COLS), F32),
            pltpu.VMEM((RANK, COLS), BF16),
            pltpu.VMEM((RANK, ROWS), BF16),
        ),
        in_specs=[anywhere] * 4,
        out_specs=(inside,) * 4,
        scratch_shapes=[
            pltpu.VMEM((TOK, ROWS), BF16),
            pltpu.VMEM((TOK, COLS), BF16),
            pltpu.VMEM((ROWS, COLS), BF16),
            pltpu.VMEM((RANK, COLS), BF16),
            pltpu.VMEM((TOK, 2 * RANK), BF16),
            pltpu.VMEM((RANK, ROWS), F32),
            pltpu.VMEM((RANK, ROWS), BF16),
            pltpu.VMEM((ROWS, COLS), BF16),
            pltpu.VMEM((2 * NX * NY, 16, STEP), BF16),
            pltpu.VMEM((NZ, 16, STEP), BF16),
            pltpu.VMEM((OWNERS, 16, STEP), BF16),
            pltpu.VMEM((RANK // 2, ROWS), BF16),
            pltpu.VMEM((RANK, ROWS), BF16),
            pltpu.VMEM((RANK, 2 * RANK), F32),
            pltpu.VMEM((RANK // 2, COLS), BF16),
            pltpu.VMEM((NY, 16, HALF), BF16),
            pltpu.VMEM((RANK, COLS), BF16),
            pltpu.VMEM((NZ, 16, HALF), BF16),
            pltpu.SemaphoreType.DMA((6,)),
            pltpu.SemaphoreType.DMA((8,)),
            pltpu.SemaphoreType.DMA((8,)),
        ],
        compiler_params=pltpu.CompilerParams(
            collective_id=0, has_side_effects=True, vmem_limit_bytes=40 << 20
        ),
        name="sums",
    )(*outside)
    results = [pltpu.with_memory_space_constraint(a, pltpu.VMEM) for a in results]
    return pl.pallas_call(
        update_kernel,
        in_specs=[inside] * 4,
        out_specs=(anywhere, anywhere),
        out_shape=(
            jax.ShapeDtypeStruct((ROWS, COLS), BF16),
            jax.ShapeDtypeStruct((RANK, COLS), F32),
        ),
        scratch_shapes=[
            pltpu.VMEM((ROWS, COLS), BF16),
            pltpu.SemaphoreType.DMA((1 + ROWS // STEP,)),
        ],
        compiler_params=pltpu.CompilerParams(vmem_limit_bytes=40 << 20),
        name="update",
    )(*results)


def solution(mesh):
    return jax.shard_map(
        body,
        mesh=mesh,
        in_specs=(P("dp", None), P("dp", "tensor"), P("dp", "tensor"), P(None, "tensor")),
        out_specs=(P("dp", "tensor"), P(None, "tensor")),
        check_vma=False,
    )
```
